128 devices in a mesh: row: 8 (over x, core), col: 16 (over y, z).
Axes of the slice: x: 4, y: 4, z: 4, core: 2. Of those that a mesh axis runs over, the one named last changes fastest.
Arguments:
- fields: float32 [5, 96, 512, 1024], P(None, None, 'col', 'row'), may hold values from -6 to 6
- heights: int32 [512, 1024], P('col', 'row'), may hold values from 0 to 24, as said below
- wall_class: int32 [96, 512, 1024], P(None, 'col', 'row'), may hold values from 0 to 3
Outputs:
- new_fields: float32 [5, 96, 512, 1024], P(None, None, 'col', 'row')
- pressure: float32 [96, 512, 1024], P(None, 'col', 'row')
The draws below stay inside these ranges and needn't reach their ends.
Inputs may be any that keep to these rules, and one draw needn't show every extreme that they name: `heights`: heights are equal within each aligned tile of 8 x 8 columns; some tile has height 24 and some has 0.
All inputs are finite; a program needn't handle non-finite values.
Results may differ from the reference program's by a relative error of at most 0.0003.
Values sent between devices are 32-bit elements; how exact they have to be, the bound alone decides.
No kernel may reach another device: no remote copies, remote signals or barrier semaphores. Data moves between devices by JAX's collectives and lax.ppermute only.
A program may use at most 256 MiB of HBM per device.

```python
import math
import jax
import jax.numpy as jnp
from jax import lax

NZ = 96
TILE = 8
HMAX = 24
NX = 512
NY = 1024


def draw_fields(key, part):
    key = jax.random.fold_in(key, 7)
    shape = (5, NZ, NX, NY)
    return jnp.clip(jax.random.normal(key, shape, jnp.float32), -6.0, 6.0)


def draw_heights(key, part):
    key = jax.random.fold_in(key, 11)
    built_key, tall_key, pick_key, other_key = jax.random.split(key, 4)
    tiles_x = NX // TILE
    tiles_y = NY // TILE
    count = tiles_x * tiles_y
    built = jax.random.randint(built_key, (tiles_x, tiles_y), 0, 5) < 2
    tall = jax.random.randint(tall_key, (tiles_x, tiles_y), 1, HMAX + 1)
    tile_heights = jnp.where(built, tall, 0)
    identity = jnp.arange(count, dtype=jnp.int32).reshape(tiles_x, tiles_y)
    highest_tile = jax.random.randint(pick_key, (), 0, count)
    empty_tile = (highest_tile + 1 + jax.random.randint(other_key, (), 0, count - 1)) % count
    tile_heights = jnp.where(identity == highest_tile, HMAX, tile_heights)
    tile_heights = jnp.where(identity == empty_tile, 0, tile_heights)
    return jnp.repeat(jnp.repeat(tile_heights, TILE, axis=0), TILE, axis=1).astype(jnp.int32)


def set_ends(values, key, low, largest):
    longest = values.shape.index(max(values.shape))
    spots = []
    for shift in (0, 1):
        where = [jax.random.randint(jax.random.fold_in(key, axis), (), 0, length) for axis, length in enumerate(values.shape)]
        where[longest] = (where[longest] + shift) % values.shape[longest]
        spots.append(tuple(where))
    return values.at[spots[0]].set(low).at[spots[1]].set(largest)


def setup_inputs(seed: int = 0) -> dict:
    keys = jax.random.split(jax.random.key(seed), 4)
    return {
        "fields": draw_fields(jax.random.fold_in(keys[3], 71), 0),
        "heights": draw_heights(jax.random.fold_in(keys[3], 71), 0),
        "wall_class": set_ends(jax.random.randint(keys[2], (NZ, NX, NY), 0, 4), jax.random.fold_in(keys[2], 1), 0, 3).astype(jnp.int32),
    }


spacing = 2.0
step_dt = 0.5
diffusivity = 0.2
drag_table = (0.0, 0.4, 0.8, 1.2)
flux_table = (0.0, 0.3, 0.6, 0.9)
wall_values = (1.0, -0.5)

def lookup(table, wall_class):
    total = jnp.zeros(wall_class.shape, jnp.float32)
    for number in range(4):
        total = total + table[number] * (wall_class == number).astype(jnp.float32)
    return total

def provisional_fields(center, east_side, west_side, north_side, south_side, heights, wall_class):
    upper_side = jnp.concatenate([center[:, 1:], center[:, -1:]], axis=1)
    lower_side = jnp.concatenate([center[:, :1], center[:, :-1]], axis=1)
    velocity_u = center[0]
    velocity_v = center[1]
    velocity_w = center[2]
    advection = (velocity_u * (east_side - west_side) + velocity_v * (north_side - south_side) + velocity_w * (upper_side - lower_side)) / (2.0 * spacing)
    laplacian = (east_side + west_side + north_side + south_side + upper_side + lower_side - 6.0 * center) / (spacing * spacing)
    speed_mag = jnp.sqrt(velocity_u * velocity_u + velocity_v * velocity_v + velocity_w * velocity_w + 0.01)
    drag_coef = lookup(drag_table, wall_class)
    flux_coef = lookup(flux_table, wall_class)
    momentum = -drag_coef * speed_mag * center[:3]
    targets = jnp.array(wall_values, jnp.float32)[:, None, None, None]
    scalar_terms = flux_coef * (targets - center[3:])
    tendency = -advection + diffusivity * laplacian + jnp.concatenate([momentum, scalar_terms], axis=0)
    levels = jnp.arange(center.shape[1], dtype=jnp.int32)[:, None, None]
    fluid_mask = (levels >= heights[None]).astype(jnp.float32)
    velocities = fluid_mask * (center[:3] + step_dt * tendency[:3])
    scalar_new = center[3:] + step_dt * fluid_mask * tendency[3:]
    return (velocities, scalar_new, fluid_mask)

def horizontal_eigen(start_x, count_x, total_x, start_y, count_y, total_y):
    wave_x = (start_x + jnp.arange(count_x, dtype=jnp.int32)).astype(jnp.float32) * (2.0 * math.pi / total_x)
    wave_y = (start_y + jnp.arange(count_y, dtype=jnp.int32)).astype(jnp.float32) * (2.0 * math.pi / total_y)
    return (2.0 * jnp.cos(wave_x)[:, None] - 2.0 + 2.0 * jnp.cos(wave_y)[None, :] - 2.0) / (spacing * spacing)

def tridiagonal(real_src, imag_src, eigen_horiz):
    inverse_sq = 1.0 / (spacing * spacing)
    depth = real_src.shape[0]
    diag_base = jnp.full((depth,), -2.0 * inverse_sq, jnp.float32)
    diag_base = diag_base.at[0].set(-inverse_sq).at[depth - 1].set(-3.0 * inverse_sq)

    def factor_step(factor_prev, base_level):
        denominator = base_level + eigen_horiz - inverse_sq * factor_prev
        factor = inverse_sq / denominator
        return (factor, (factor, denominator))
    unused, (factors, denominators) = lax.scan(factor_step, jnp.zeros_like(eigen_horiz), diag_base, unroll=8)

    def forward(reduced_prev, inputs):
        real_level, imag_level, denominator = inputs
        real_red = (real_level - inverse_sq * reduced_prev[0]) / denominator
        imag_red = (imag_level - inverse_sq * reduced_prev[1]) / denominator
        return ((real_red, imag_red), (real_red, imag_red))
    initial = (jnp.zeros_like(real_src[0]), jnp.zeros_like(imag_src[0]))
    unused_red, (real_all, imag_all) = lax.scan(forward, initial, (real_src, imag_src, denominators), unroll=8)

    def backward(above_val, inputs):
        factor, real_red, imag_red = inputs
        current = (real_red - factor * above_val[0], imag_red - factor * above_val[1])
        return (current, current)
    unused_last, (real_out, imag_out) = lax.scan(backward, initial, (factors, real_all, imag_all), reverse=True, unroll=8)
    return (real_out, imag_out)

def reference(fields, heights, wall_class):
    east_side = jnp.roll(fields, -1, 2)
    west_side = jnp.roll(fields, 1, 2)
    north_side = jnp.roll(fields, -1, 3)
    south_side = jnp.roll(fields, 1, 3)
    velocities, scalar_new, fluid_mask = provisional_fields(fields, east_side, west_side, north_side, south_side, heights, wall_class)
    prov_u = velocities[0]
    prov_v = velocities[1]
    prov_w = velocities[2]
    w_prev = jnp.concatenate([jnp.zeros_like(prov_w[:1]), prov_w[:-1]], axis=0)
    source = (prov_u - jnp.roll(prov_u, 1, 1) + (prov_v - jnp.roll(prov_v, 1, 2)) + (prov_w - w_prev)) / (spacing * step_dt)
    total_x = source.shape[1]
    total_y = source.shape[2]
    transformed = jnp.fft.fft2(source, axes=(1, 2))
    eigen_horiz = horizontal_eigen(0, total_x, total_x, 0, total_y, total_y)
    real_out, imag_out = tridiagonal(jnp.real(transformed), jnp.imag(transformed), eigen_horiz)
    pressure = jnp.real(jnp.fft.ifft2(lax.complex(real_out, imag_out), axes=(1, 2)))
    grad_x = (jnp.roll(pressure, -1, 1) - pressure) / spacing
    grad_y = (jnp.roll(pressure, -1, 2) - pressure) / spacing
    grad_z = jnp.concatenate([pressure[1:] - pressure[:-1], -2.0 * pressure[-1:]], axis=0) / spacing
    corrected = fluid_mask * (velocities - step_dt * jnp.stack([grad_x, grad_y, grad_z], axis=0))
    new_fields = jnp.concatenate([corrected, scalar_new], axis=0)
    return (new_fields, pressure)
```

```python
import functools
import math

import jax
import jax.numpy as jnp
import ml_dtypes
import numpy as np
from jax import lax
from jax.experimental import pallas as pl
from jax.experimental.pallas import tpu as pltpu
from jax.sharding import PartitionSpec as P

NZ, BX, BY = 96, 32, 128
CX, RY = 16, 8
ND = CX * RY
CHUNK = 8
PARTS = NZ // CHUNK
bf16 = jnp.bfloat16
f32 = jnp.float32
VMEM_LIMIT = 56 * 1024 * 1024


def halves(matrix):
    high = matrix.astype(ml_dtypes.bfloat16)
    low = (matrix - high.astype(np.float64)).astype(ml_dtypes.bfloat16)
    return high, low


def right_stack(matrix):
    high, low = halves(matrix)
    return np.block([[high, low], [high, np.zeros_like(low)]])


def left_stack(matrix):
    high, low = halves(matrix)
    return np.block([[high, high], [low, np.zeros_like(low)]])


def wide_stack(matrix):
    high, low = halves(matrix)
    return np.concatenate([high, low], axis=1)


def cas(angle):
    return np.cos(angle) + np.sin(angle)


def block_tables():
    levels = np.arange(NZ) + 0.5
    vertical = np.sqrt(2.0 / NZ) * np.cos(np.pi * np.outer(levels, levels) / NZ)
    waves = np.arange(BY)
    sines = np.sin(np.pi * np.outer(waves, waves) / BY)
    to_waves = sines.copy()
    to_waves[0, 0] = 1.0
    from_waves = sines * (2.0 / BY)
    edge_rows = from_waves.copy()
    from_waves[0, 0] = 1.0
    diagonal = (
        2.0
        + (2.0 - 2.0 * np.cos(np.pi * levels / NZ))[:, None]
        + (2.0 - 2.0 * np.cos(np.pi * waves / BY))[None, :]
    )
    edges = np.zeros((BY, BY))
    edges[:, 0] = edge_rows[:, 1]
    edges[0, 0] = 1.0
    edges[:, BX] = edge_rows[:, BY - 1]
    near = sines[1].copy()
    far = sines[BY - 1].copy()
    return dict(
        vertical=left_stack(vertical),
        vertical_right=right_stack(vertical),
        to_waves=right_stack(to_waves),
        plain_sines=right_stack(sines),
        edge_rows=right_stack(edge_rows),
        from_waves=right_stack(from_waves),
        edges=right_stack(edges),
        diagonal=diagonal.astype(np.float32),
        near_far=np.stack([near, far] + [np.zeros(BY)] * 6).astype(np.float32),
    )


def skeleton_tables():
    total_x, total_y = CX * BX, RY * BY
    grid = np.zeros((RY, CX, CX, RY))
    a0, c = np.arange(CX), np.arange(CX)
    b0, r = np.arange(RY), np.arange(RY)
    part_x = cas(2 * np.pi * np.outer(a0, c) / CX)
    part_y = cas(2 * np.pi * np.outer(b0, r) / RY)
    grid = np.einsum("ac,br->bacr", part_x, part_y)
    mirrored = grid[:, -a0 % CX]
    grid = grid.reshape(ND, ND)
    mirrored = mirrored.reshape(ND, ND)
    j, i = np.arange(BY), np.arange(BX)
    b1, a1 = np.arange(BY), np.arange(BX)
    y_forward, y_inverse = [], []
    for b in range(RY):
        angle = 2 * np.pi * np.outer(j, b + RY * b1) / total_y
        y_forward.append(np.concatenate([np.cos(angle), np.sin(angle)]))
        angle_other = 2 * np.pi * np.outer(j, (-b) % RY + RY * b1) / total_y
        y_inverse.append(np.concatenate([np.cos(angle).T, np.sin(angle_other).T]))
    x_forward, x_inverse = [], []
    for a in range(CX):
        angle = 2 * np.pi * np.outer(i, a + CX * a1) / total_x
        x_forward.append(np.concatenate([np.cos(angle), np.sin(angle)]))
        angle_other = 2 * np.pi * np.outer(i, (-a) % CX + CX * a1) / total_x
        x_inverse.append(np.concatenate([np.cos(angle).T, np.sin(angle_other).T]))

    def lanes(blocks):
        matrix = np.concatenate(blocks)
        out = np.concatenate(halves(matrix), axis=1)
        return np.concatenate([out, np.zeros((out.shape[0], 64), out.dtype)], axis=1)

    lane = np.arange(ND)
    lane_b0, lane_a0 = lane // CX, lane % CX
    wave_x = lane_a0[None, :] + CX * a1[:, None]
    wave_y = lane_b0[None, :] + RY * b1[:, None]
    swap = np.zeros((ND, ND))
    swap[(lane_b0 * CX + (-lane_a0) % CX), lane] = 1.0
    return dict(
        grid=left_stack(grid),
        mirrored=left_stack(mirrored),
        grid_back=left_stack(grid.T / (total_x * total_y)),
        y_forward=np.stack([wide_stack(m) for m in y_forward]),
        y_inverse=np.stack([wide_stack(m) for m in y_inverse]),
        x_forward=lanes(x_forward),
        x_inverse=lanes(x_inverse),
        swap=swap.astype(ml_dtypes.bfloat16),
        eigen_x=(2 - 2 * np.cos(2 * np.pi * wave_x / total_x)).astype(np.float32),
        eigen_y=(2 - 2 * np.cos(2 * np.pi * wave_y / total_y)).astype(np.float32),
    )


def split(values):
    high = values.astype(bf16)
    return high, (values - high.astype(f32)).astype(bf16)


def dot(left, right):
    return jnp.dot(left, right, preferred_element_type=f32)


def times_right(values, stack):
    out = dot(jnp.concatenate(split(values), axis=1), stack)
    half = out.shape[1] // 2
    return out[:, :half] + out[:, half:]


def times_left(stack, values):
    out = dot(stack, jnp.concatenate(split(values), axis=0))
    half = out.shape[0] // 2
    return out[:half] + out[half:]


def lane_index(rows):
    return lax.broadcasted_iota(jnp.int32, (rows, BY), 1)


def row_index(rows):
    return lax.broadcasted_iota(jnp.int32, (rows, BY), 0)


def edge_kernel(field, first_x, last_x, first_y, last_y):
    rows = field.at[0].reshape(NZ * BX, BY)
    first_x[0] = rows[pl.ds(0, NZ, stride=BX), :]
    last_x[0] = rows[pl.ds(BX - 1, NZ, stride=BX), :]
    lane = lane_index(BX)

    def step(level, carry):
        first, last = carry
        turned = pltpu.roll(field[0, level], level, axis=1)
        first = jnp.where(lane == level, turned, first)
        last = jnp.where(lane == lax.rem(level + BY - 1, BY), turned, last)
        return first, last

    zero = jnp.zeros((BX, BY), f32)
    first, last = lax.fori_loop(0, NZ, step, (zero, zero), unroll=4)
    first_y[0] = first
    last_y[0] = last


def block_edges(fields):
    plane = pl.BlockSpec((1, NZ, BY), lambda n: (n, 0, 0))
    packed = pl.BlockSpec((1, BX, BY), lambda n: (n, 0, 0))
    return pl.pallas_call(
        edge_kernel,
        grid=(5,),
        in_specs=[pl.BlockSpec((1, NZ, BX, BY), lambda n: (n, 0, 0, 0))],
        out_specs=[plane, plane, packed, packed],
        out_shape=[jax.ShapeDtypeStruct((5, NZ, BY), f32)] * 2
        + [jax.ShapeDtypeStruct((5, BX, BY), f32)] * 2,
        compiler_params=pltpu.CompilerParams(vmem_limit_bytes=VMEM_LIMIT),
    )(fields)


def eliminate(rhs_of, diagonal, factors, reduced):
    def forward(index, carry):
        factor_prev, reduced_prev = carry
        factor = 1.0 / (diagonal[...] - factor_prev)
        value = factor * (rhs_of(index) + reduced_prev)
        factors[index] = factor
        reduced[index] = value
        return factor, value

    zero = jnp.zeros((NZ, BY), f32)
    lax.fori_loop(0, BX - 1, forward, (zero, zero))

    def backward(step, above):
        index = BX - 2 - step
        value = reduced[index] + factors[index] * above
        reduced[index] = value
        return value

    lax.fori_loop(0, BX - 1, backward, zero)


def source_kernel(
    fields_hbm,
    wall_hbm,
    heights,
    west,
    east,
    south,
    north,
    vertical,
    vertical_right,
    to_waves,
    edge_rows,
    edges,
    diagonal,
    new_hbm,
    waves,
    condensed,
    fields,
    wall,
    new,
    source,
    factors,
    reduced,
    in_sem,
    wall_sem,
    out_sem,
):
    def field_copy(part):
        levels = pl.ds(part * CHUNK, CHUNK)
        return pltpu.make_async_copy(
            fields_hbm.at[:, levels], fields.at[:, levels], in_sem.at[part]
        )

    def wall_copy(part):
        levels = pl.ds(part * CHUNK, CHUNK)
        return pltpu.make_async_copy(wall_hbm.at[levels], wall.at[levels], wall_sem.at[part])

    def new_copy(part):
        levels = pl.ds(part * CHUNK, CHUNK)
        return pltpu.make_async_copy(new.at[:, levels], new_hbm.at[:, levels], out_sem.at[part])

    for part in range(PARTS):
        field_copy(part).start()
        wall_copy(part).start()
    field_copy(0).wait()

    lane = lane_index(BX)
    row = row_index(BX)
    zero = jnp.zeros((BX, BY), f32)

    def level_step(level, carry):
        w_below, v_edge = carry
        below = jnp.maximum(level - 1, 0)
        above = jnp.minimum(level + 1, NZ - 1)
        u, v, w = fields[0, level], fields[1, level], fields[2, level]
        fluid = jnp.where(level >= heights[...], 1.0, 0.0).astype(f32)
        carried = fluid * 0.125
        mixed = fluid * 0.025
        u_part, v_part, w_part = u * carried, v * carried, w * carried
        c_east, c_west = mixed - u_part, mixed + u_part
        c_north, c_south = mixed - v_part, mixed + v_part
        c_up, c_down = mixed - w_part, mixed + w_part
        speed = jnp.sqrt(u * u + v * v + w * w + 0.01)
        classes = wall[level].astype(f32)
        own_velocity = fluid * (0.85 - 0.2 * classes * speed)
        flux = fluid * (0.15 * classes)
        own_scalar = 1.0 - fluid * 0.15 - flux
        results = []
        for number in range(5):
            f = fields[number, level]
            f_east = jnp.where(
                row == BX - 1,
                east[number, pl.ds(level, 1)],
                pltpu.roll(f, BX - 1, axis=0),
            )
            f_west = jnp.where(row == 0, west[number, pl.ds(level, 1)], pltpu.roll(f, 1, axis=0))
            shift_north = lax.rem(BY - 1 - level + BY, BY)
            f_north = jnp.where(
                lane == BY - 1,
                pltpu.roll(north[number], shift_north, axis=1),
                pltpu.roll(f, BY - 1, axis=1),
            )
            shift_south = lax.rem(BY + 1 - level, BY)
            f_south = jnp.where(
                lane == 0,
                pltpu.roll(south[number], shift_south, axis=1),
                pltpu.roll(f, 1, axis=1),
            )
            total = (
                (c_east * f_east + c_west * f_west)
                + (c_north * f_north + c_south * f_south)
                + (c_up * fields[number, above] + c_down * fields[number, below])
            )
            if number < 3:
                total = total + own_velocity * f
            else:
                total = total + own_scalar * f + (1.0 if number == 3 else -0.5) * flux
            new[number, level] = total
            results.append(total)
        u_new, v_new, w_new = results[:3]
        u_behind = jnp.where(row == 0, 0.0, pltpu.roll(u_new, 1, axis=0))
        v_behind = jnp.where(lane == 0, 0.0, pltpu.roll(v_new, 1, axis=1))
        divergence = (u_new - u_behind) + (v_new - v_behind) + (w_new - w_below)
        source[pl.ds(level, BX, stride=NZ), :] = -4.0 * divergence
        source[pl.ds(BX * NZ + level, 1), :] = 4.0 * u_new[BX - 1 :]
        v_edge = jnp.where(lane == level, pltpu.roll(v_new, level + 1, axis=1), v_edge)
        return w_new, v_edge

    def part_step(part, carry):
        @pl.when(part < PARTS - 1)
        def _():
            field_copy(part + 1).wait()

        wall_copy(part).wait()
        carry = lax.fori_loop(part * CHUNK, (part + 1) * CHUNK, level_step, carry)
        new_copy(part).start()
        return carry

    _, v_edge = lax.fori_loop(0, PARTS, part_step, (zero, zero))

    for i in range(1, BX):
        along_y = times_right(source[i * NZ : (i + 1) * NZ, :], to_waves[...])
        waves[i - 1] = times_left(vertical[...], along_y)
    own_x = times_left(vertical[...], source[0:NZ, :])
    next_x = times_left(vertical[...], source[BX * NZ : (BX + 1) * NZ, :])

    eliminate(lambda index: waves[index], diagonal, factors, reduced)

    own_x = own_x + times_right(reduced[0], edge_rows[...])
    next_x = next_x + times_right(reduced[BX - 2], edge_rows[...])
    lane_z = lane_index(NZ)
    next_y = times_right(4.0 * v_edge[:, :NZ], vertical_right[...])
    packed = jnp.concatenate([zero[:, :NZ], next_y, jnp.zeros((2 * BX, NZ), f32)], axis=0).T
    for i in range(1, BX):
        merged = jnp.where(lane_z == 0, waves[i - 1], reduced[i - 1])
        ends = pltpu.roll(times_right(merged, edges[...]), i, axis=1)
        packed = packed + jnp.where((lane_z == i) | (lane_z == BX + i), ends, 0.0)
    condensed[pl.ds(0, NZ, stride=3), :] = own_x
    condensed[pl.ds(1, NZ, stride=3), :] = next_x
    condensed[pl.ds(2, NZ, stride=3), :] = packed
    condensed[3 * NZ :, :] = jnp.zeros((3 * (ND - NZ), BY), f32)

    for part in range(PARTS):
        new_copy(part).wait()


vmem_spec = pl.BlockSpec(memory_space=pltpu.VMEM)
any_spec = pl.BlockSpec(memory_space=pl.ANY)


def condensed_source(fields, wall_class, heights, west, east, south, north, tables):
    return pl.pallas_call(
        source_kernel,
        in_specs=[any_spec, any_spec] + [vmem_spec] * 11,
        out_specs=[any_spec, vmem_spec, vmem_spec],
        out_shape=[
            jax.ShapeDtypeStruct((5, NZ, BX, BY), f32),
            jax.ShapeDtypeStruct((BX - 1, NZ, BY), f32),
            jax.ShapeDtypeStruct((3 * ND, BY), f32),
        ],
        scratch_shapes=[
            pltpu.VMEM((5, NZ, BX, BY), f32),
            pltpu.VMEM((NZ, BX, BY), jnp.int32),
            pltpu.VMEM((5, NZ, BX, BY), f32),
            pltpu.VMEM(((BX + 1) * NZ, BY), f32),
            pltpu.VMEM((BX - 1, NZ, BY), f32),
            pltpu.VMEM((BX - 1, NZ, BY), f32),
            pltpu.SemaphoreType.DMA((PARTS,)),
            pltpu.SemaphoreType.DMA((PARTS,)),
            pltpu.SemaphoreType.DMA((PARTS,)),
        ],
        compiler_params=pltpu.CompilerParams(vmem_limit_bytes=VMEM_LIMIT),
    )(
        fields,
        wall_class,
        heights,
        west,
        east,
        south,
        north,
        tables["vertical"],
        tables["vertical_right"],
        tables["to_waves"],
        tables["edge_rows"],
        tables["edges"],
        tables["diagonal"],
    )


def blockwise(values, stacks):
    parts = []
    for b in range(RY):
        other = (-b) % RY
        pair = jnp.concatenate(
            [values[b * CX : (b + 1) * CX], values[other * CX : (other + 1) * CX]], axis=1
        )
        out = dot(jnp.concatenate(split(pair), axis=0), stacks[b])
        parts.append(out[:CX, :BY] + out[:CX, BY:] + out[CX:, :BY])
    return jnp.concatenate(parts, axis=0)


def per_column(values, mirrored, table):
    pair = values + pltpu.roll(mirrored, BX, axis=1)
    pair = pair + pltpu.roll(pair, 2 * BX, axis=1)
    lane, row = lane_index(ND), row_index(ND)
    mine = lax.rem(row, CX)
    wide = jnp.concatenate(
        [jnp.where(mine == 2 * q + lane // 64, pair, 0.0) for q in range(CX // 2)], axis=1
    )
    out = dot(jnp.concatenate(split(wide), axis=0), table)
    top, bottom = out[:ND], out[ND:]
    out = top + pltpu.roll(top, BY - BX, axis=1) + bottom
    return jnp.where(lane < BX, out, 0.0)


def skeleton_kernel(
    mode_eigen,
    received,
    grid,
    mirrored,
    grid_back,
    y_forward,
    y_inverse,
    x_forward,
    x_inverse,
    swap,
    eigen_x,
    eigen_y,
    answer,
):
    own_x = received[pl.ds(0, ND, stride=3), :]
    next_x = received[pl.ds(1, ND, stride=3), :]
    lines_y = received[pl.ds(2, ND, stride=3), :]
    lane = lane_index(ND)
    lines_x = own_x + pltpu.roll(next_x, RY, axis=0)
    before = pltpu.roll(lines_y, BY - BX, axis=1).reshape(CX, RY, BY)
    before = pltpu.roll(before, 1, axis=1).reshape(ND, BY)
    lines_y = jnp.where(lane < BX, lines_y + before, 0.0)

    both = times_left(grid[...], jnp.concatenate([lines_x, lines_y], axis=1))
    turned = times_left(mirrored[...], lines_y)
    spec_x = blockwise(both[:, :BY], y_forward).T
    spec_y = per_column(both[:, BY:], turned, x_forward[...]).T

    base = eigen_y[...] + mode_eigen[0]
    total_x = jnp.zeros((BY, ND), f32)
    sums = []
    for a in range(BX):
        value = (spec_x + spec_y[a : a + 1]) / (base + eigen_x[a : a + 1])
        total_x = total_x + value
        sums.append(jnp.sum(value, axis=0, keepdims=True))
    total_y = jnp.concatenate(sums, axis=0)
    high, low = split(total_y)
    turned = dot(high, swap[...]) + dot(low, swap[...])
    fill = jnp.zeros((ND - BX, ND), f32)
    total_y = jnp.concatenate([total_y, fill], axis=0).T
    turned = jnp.concatenate([turned, fill], axis=0).T
    lines_x = blockwise(total_x.T, y_inverse)
    lines_y = per_column(total_y, turned, x_inverse[...])
    both = times_left(grid_back[...], jnp.concatenate([lines_x, lines_y], axis=1))
    own_x, own_y = both[:, :BY], both[:, BY:]
    next_x = pltpu.roll(own_x, ND - RY, axis=0)
    next_y = pltpu.roll(own_y.reshape(CX, RY, BY), RY - 1, axis=1).reshape(ND, BY)
    answer[pl.ds(0, ND, stride=3), :] = own_x
    answer[pl.ds(1, ND, stride=3), :] = next_x
    answer[pl.ds(2, ND, stride=3), :] = own_y + pltpu.roll(next_y, BX, axis=1)


def skeleton_solve(received, mode_eigen, tables):
    return pl.pallas_call(
        skeleton_kernel,
        in_specs=[pl.BlockSpec(memory_space=pltpu.SMEM)] + [vmem_spec] * 11,
        out_specs=vmem_spec,
        out_shape=jax.ShapeDtypeStruct((3 * ND, BY), f32),
        compiler_params=pltpu.CompilerParams(vmem_limit_bytes=VMEM_LIMIT),
    )(
        mode_eigen,
        received,
        tables["grid"],
        tables["mirrored"],
        tables["grid_back"],
        tables["y_forward"],
        tables["y_inverse"],
        tables["x_forward"],
        tables["x_inverse"],
        tables["swap"],
        tables["eigen_x"],
        tables["eigen_y"],
    )


def correct_kernel(
    before_hbm,
    waves,
    answer,
    heights,
    vertical,
    vertical_right,
    plain_sines,
    from_waves,
    diagonal,
    near_far,
    new_hbm,
    pressure_hbm,
    velocity,
    planes,
    pressure,
    factors,
    reduced,
    in_sem,
    out_sem,
    pressure_sem,
):
    def in_copy(part):
        levels = pl.ds(part * CHUNK, CHUNK)
        return pltpu.make_async_copy(
            before_hbm.at[pl.ds(0, 3), levels], velocity.at[:, levels], in_sem.at[part]
        )

    def out_copy(part):
        levels = pl.ds(part * CHUNK, CHUNK)
        return pltpu.make_async_copy(
            velocity.at[:, levels], new_hbm.at[pl.ds(0, 3), levels], out_sem.at[part]
        )

    def pressure_copy(part):
        levels = pl.ds(part * CHUNK, CHUNK)
        return pltpu.make_async_copy(
            pressure.at[levels], pressure_hbm.at[levels], pressure_sem.at[part]
        )

    for part in range(PARTS):
        in_copy(part).start()

    own_x = answer[pl.ds(0, NZ, stride=3), :]
    next_x = answer[pl.ds(1, NZ, stride=3), :]
    lines_y = answer[pl.ds(2, NZ, stride=3), :]
    lane_z = lane_index(NZ)
    near, far = near_far[0:1], near_far[1:2]
    for i in range(1, BX):
        rhs = waves[i - 1] + lines_y[:, i : i + 1] * near + lines_y[:, BX + i : BX + i + 1] * far
        if i == 1:
            rhs = rhs + times_right(own_x, plain_sines[...])
        if i == BX - 1:
            rhs = rhs + times_right(next_x, plain_sines[...])
        reduced[i - 1] = rhs
    eliminate(lambda index: reduced[index], diagonal, factors, reduced)

    planes[0:NZ, :] = times_left(vertical[...], own_x)
    planes[BX * NZ : (BX + 1) * NZ, :] = times_left(vertical[...], next_x)
    for i in range(1, BX):
        merged = jnp.where(lane_z == 0, lines_y[:, i : i + 1], reduced[i - 1])
        along_y = times_right(merged, from_waves[...])
        planes[i * NZ : (i + 1) * NZ, :] = times_left(vertical[...], along_y)
    tall = jnp.concatenate([lines_y, jnp.zeros((BY - NZ, BY), f32)], axis=0).T
    north = times_right(tall[BX : 2 * BX, :NZ], vertical_right[...])
    north = jnp.concatenate([north, jnp.zeros((BX, BY - NZ), f32)], axis=1)

    lane = lane_index(BX)

    def level_step(level, here):
        above_level = jnp.minimum(level + 1, NZ - 1)
        above = planes[pl.ds(above_level, BX, stride=NZ), :]
        above = jnp.where(level == NZ - 1, -here, above)
        east = planes[pl.ds(NZ + level, BX, stride=NZ), :]
        shift = lax.rem(BY - 1 - level + BY, BY)
        side = jnp.where(
            lane == BY - 1, pltpu.roll(north, shift, axis=1), pltpu.roll(here, BY - 1, axis=1)
        )
        factor = jnp.where(level >= heights[...], 0.25, 0.0).astype(f32)
        velocity[0, level] = velocity[0, level] - factor * (east - here)
        velocity[1, level] = velocity[1, level] - factor * (side - here)
        velocity[2, level] = velocity[2, level] - factor * (above - here)
        pressure[level] = here
        return above

    def part_step(part, here):
        in_copy(part).wait()
        here = lax.fori_loop(part * CHUNK, (part + 1) * CHUNK, level_step, here)
        out_copy(part).start()
        pressure_copy(part).start()
        return here

    lax.fori_loop(0, PARTS, part_step, planes[pl.ds(0, BX, stride=NZ), :])
    for part in range(PARTS):
        out_copy(part).wait()
        pressure_copy(part).wait()


def corrected(before, waves, answer, heights, tables):
    return pl.pallas_call(
        correct_kernel,
        in_specs=[any_spec] + [vmem_spec] * 9,
        out_specs=[any_spec, any_spec],
        out_shape=[
            jax.ShapeDtypeStruct((5, NZ, BX, BY), f32),
            jax.ShapeDtypeStruct((NZ, BX, BY), f32),
        ],
        scratch_shapes=[
            pltpu.VMEM((3, NZ, BX, BY), f32),
            pltpu.VMEM(((BX + 1) * NZ, BY), f32),
            pltpu.VMEM((NZ, BX, BY), f32),
            pltpu.VMEM((BX - 1, NZ, BY), f32),
            pltpu.VMEM((BX - 1, NZ, BY), f32),
            pltpu.SemaphoreType.DMA((PARTS,)),
            pltpu.SemaphoreType.DMA((PARTS,)),
            pltpu.SemaphoreType.DMA((PARTS,)),
        ],
        input_output_aliases={0: 0},
        compiler_params=pltpu.CompilerParams(vmem_limit_bytes=VMEM_LIMIT),
    )(
        before,
        waves,
        answer,
        heights,
        tables["vertical"],
        tables["vertical_right"],
        tables["plain_sines"],
        tables["from_waves"],
        tables["diagonal"],
        tables["near_far"],
    )


def ring(value, axis, step):
    count = lax.axis_size(axis)
    return lax.ppermute(value, axis, [(n, (n + step) % count) for n in range(count)])


def on_device(fields, heights, wall_class):
    block = {name: jnp.asarray(table) for name, table in block_tables().items()}
    skeleton = {name: jnp.asarray(table) for name, table in skeleton_tables().items()}
    first_x, last_x, first_y, last_y = block_edges(fields)
    west = ring(last_x, "col", 1)
    east = ring(first_x, "col", -1)
    south = ring(last_y, "row", 1)
    north = ring(first_y, "row", -1)
    before, waves, condensed = condensed_source(
        fields, wall_class, heights, west, east, south, north, block
    )
    received = lax.all_to_all(condensed, ("col", "row"), 0, 0, tiled=True)
    mode = lax.axis_index("col") * RY + lax.axis_index("row")
    eigen = 2.0 - 2.0 * np.cos(np.pi * (np.arange(ND) + 0.5) / NZ)
    eigen[NZ:] = 1.0
    mode_eigen = lax.dynamic_slice(jnp.asarray(eigen.astype(np.float32)), (mode,), (1,))
    solved = skeleton_solve(received, mode_eigen, skeleton)
    answer = lax.all_to_all(solved, ("col", "row"), 0, 0, tiled=True)
    return tuple(corrected(before, waves, answer, heights, block))


def solution(mesh):
    in_specs = (P(None, None, "col", "row"), P("col", "row"), P(None, "col", "row"))
    out_specs = (P(None, None, "col", "row"), P(None, "col", "row"))
    return jax.shard_map(
        on_device, mesh=mesh, in_specs=in_specs, out_specs=out_specs, check_vma=False
    )
```

```python
import functools
import math

import jax
import jax.numpy as jnp
import ml_dtypes
import numpy as np
from jax import lax
from jax.experimental import pallas as pl
from jax.experimental.pallas import tpu as pltpu
from jax.sharding import PartitionSpec as P

NZ, BX, BY = 96, 32, 128
CX, RY = 16, 8
ND = CX * RY
CHUNK = 8
ROWS = BX + 16
TALL = BX + 8
PARTS = NZ // CHUNK
bf16 = jnp.bfloat16
f32 = jnp.float32
GRANT = 64 * 1024 * 1024


def halves(matrix):
    high = matrix.astype(ml_dtypes.bfloat16)
    low = (matrix - high.astype(np.float64)).astype(ml_dtypes.bfloat16)
    return high, low


def right_stack(matrix):
    high, low = halves(matrix)
    return np.block([[high, low], [high, np.zeros_like(low)]])


def left_stack(matrix):
    high, low = halves(matrix)
    return np.block([[high, high], [low, np.zeros_like(low)]])


def wide_stack(matrix):
    high, low = halves(matrix)
    return np.concatenate([high, low], axis=1)


def cas(angle):
    return np.cos(angle) + np.sin(angle)


def block_tables():
    levels = np.arange(NZ) + 0.5
    vertical = np.sqrt(2.0 / NZ) * np.cos(np.pi * np.outer(levels, levels) / NZ)
    waves = np.arange(BY)
    sines = np.sin(np.pi * np.outer(waves, waves) / BY)
    to_waves = sines.copy()
    to_waves[0, 0] = 1.0
    from_waves = sines * (2.0 / BY)
    edge_rows = from_waves.copy()
    from_waves[0, 0] = 1.0
    diagonal = (
        2.0
        + (2.0 - 2.0 * np.cos(np.pi * levels / NZ))[:, None]
        + (2.0 - 2.0 * np.cos(np.pi * waves / BY))[None, :]
    )
    factors = [np.zeros((NZ, BY))]
    for _ in range(1, BX):
        factors.append(1.0 / (diagonal - factors[-1]))
    edges = np.zeros((BY, BY))
    edges[:, 0] = edge_rows[:, 1]
    edges[0, 0] = 1.0
    edges[:, BX] = edge_rows[:, BY - 1]
    near = sines[1].copy()
    far = sines[BY - 1].copy()
    return dict(
        vertical=left_stack(vertical),
        vertical_right=right_stack(vertical),
        to_waves=right_stack(to_waves),
        plain_sines=right_stack(sines),
        edge_rows=right_stack(edge_rows),
        from_waves=right_stack(from_waves),
        edges=right_stack(edges),
        factors=np.stack(factors[1:]).astype(np.float32),
        near_far=np.stack([near, far] + [np.zeros(BY)] * 6).astype(np.float32),
    )


def skeleton_tables():
    total_x, total_y = CX * BX, RY * BY
    grid = np.zeros((RY, CX, CX, RY))
    a0, c = np.arange(CX), np.arange(CX)
    b0, r = np.arange(RY), np.arange(RY)
    part_x = cas(2 * np.pi * np.outer(a0, c) / CX)
    part_y = cas(2 * np.pi * np.outer(b0, r) / RY)
    grid = np.einsum("ac,br->bacr", part_x, part_y)
    mirrored = grid[:, -a0 % CX]
    grid = grid.reshape(ND, ND)
    mirrored = mirrored.reshape(ND, ND)
    j, i = np.arange(BY), np.arange(BX)
    b1, a1 = np.arange(BY), np.arange(BX)
    y_forward, y_inverse = [], []
    for b in range(RY):
        angle = 2 * np.pi * np.outer(j, b + RY * b1) / total_y
        y_forward.append(np.concatenate([np.cos(angle), np.sin(angle)]))
        angle_other = 2 * np.pi * np.outer(j, (-b) % RY + RY * b1) / total_y
        y_inverse.append(np.concatenate([np.cos(angle).T, np.sin(angle_other).T]))
    x_forward, x_inverse = [], []
    for a in range(CX):
        angle = 2 * np.pi * np.outer(i, a + CX * a1) / total_x
        x_forward.append(np.concatenate([np.cos(angle), np.sin(angle)]))
        angle_other = 2 * np.pi * np.outer(i, (-a) % CX + CX * a1) / total_x
        x_inverse.append(np.concatenate([np.cos(angle).T, np.sin(angle_other).T]))

    def lanes(blocks):
        matrix = np.concatenate(blocks)
        out = np.concatenate(halves(matrix), axis=1)
        return np.concatenate([out, np.zeros((out.shape[0], 64), out.dtype)], axis=1)

    lane = np.arange(ND)
    lane_b0, lane_a0 = lane // CX, lane % CX
    wave_x = lane_a0[None, :] + CX * a1[:, None]
    wave_y = lane_b0[None, :] + RY * b1[:, None]
    swap = np.zeros((ND, ND))
    swap[(lane_b0 * CX + (-lane_a0) % CX), lane] = 1.0
    return dict(
        grid=left_stack(grid),
        mirrored=left_stack(mirrored),
        grid_back=left_stack(grid.T / (total_x * total_y)),
        y_forward=np.stack([wide_stack(m) for m in y_forward]),
        y_inverse=np.stack([wide_stack(m) for m in y_inverse]),
        x_forward=lanes(x_forward),
        x_inverse=lanes(x_inverse),
        swap=swap.astype(ml_dtypes.bfloat16),
        eigen_x=(2 - 2 * np.cos(2 * np.pi * wave_x / total_x)).astype(np.float32),
        eigen_y=(2 - 2 * np.cos(2 * np.pi * wave_y / total_y)).astype(np.float32),
    )


def split(values):
    high = values.astype(bf16)
    return high, (values - high.astype(f32)).astype(bf16)


def dot(left, right):
    return jnp.dot(left, right, preferred_element_type=f32)


def times_right(values, stack):
    out = dot(jnp.concatenate(split(values), axis=1), stack)
    half = out.shape[1] // 2
    return out[:, :half] + out[:, half:]


def times_left(stack, values):
    out = dot(stack, jnp.concatenate(split(values), axis=0))
    half = out.shape[0] // 2
    return out[:half] + out[half:]


def lane_index(rows):
    return lax.broadcasted_iota(jnp.int32, (rows, BY), 1)


def row_index(rows):
    return lax.broadcasted_iota(jnp.int32, (rows, BY), 0)


def edge_kernel(fields, first_x, last_x, first_y, last_y, held, west, east, south, north, *sems):
    sem, out_sem = sems

    def copy(number):
        return pltpu.make_async_copy(fields.at[number], held.at[number], sem.at[number])

    for number in range(5):
        copy(number).start()
    lane = lane_index(BX)

    def step(number, carry):
        copy(number).wait()
        rows = held.at[number].reshape(NZ * BX, BY)
        east[pl.ds(pl.multiple_of(number * NZ, NZ), NZ), :] = rows[pl.ds(0, NZ, stride=BX), :]
        west[pl.ds(pl.multiple_of(number * NZ, NZ), NZ), :] = rows[pl.ds(BX - 1, NZ, stride=BX), :]
        for group in range(2):
            first, last = jnp.zeros((BX, BY), f32), jnp.zeros((BX, BY), f32)
            for level in range(NZ // 2):
                turned = held[number, group * (NZ // 2) + level]
                if level:
                    turned = pltpu.roll(turned, 2 * level, axis=1)
                first = jnp.where(lane == 2 * level, turned, first)
                last = jnp.where(lane == (2 * level - 1) % BY, turned, last)
            north[2 * number + group] = first
            south[2 * number + group] = last
        return carry

    lax.fori_loop(0, 5, step, 0)
    for copied in fetches(
        [east, west, north, south], [first_x, last_x, first_y, last_y], out_sem
    ):
        copied.wait()


def block_edges(fields):
    plane = (5 * NZ, BY)
    packed = (10, BX, BY)
    shapes = [plane, plane, packed, packed]
    return pl.pallas_call(
        edge_kernel,
        in_specs=[any_spec],
        out_specs=[any_spec] * 4,
        out_shape=[jax.ShapeDtypeStruct(shape, f32) for shape in shapes],
        scratch_shapes=[pltpu.VMEM((5, NZ, BX, BY), f32)]
        + [pltpu.VMEM(shape, f32) for shape in shapes]
        + [pltpu.SemaphoreType.DMA((5,)), pltpu.SemaphoreType.DMA((4,))],
        compiler_params=pltpu.CompilerParams(vmem_limit_bytes=GRANT),
    )(fields)


def eliminate(rhs, factors, reduced):
    def forward(index, reduced_prev):
        value = factors[index] * (rhs[index] + reduced_prev)
        reduced[index] = value
        return value

    zero = jnp.zeros((NZ, BY), f32)
    lax.fori_loop(0, BX - 1, forward, zero, unroll=True)

    def backward(step, above):
        index = BX - 2 - step
        value = reduced[index] + factors[index] * above
        reduced[index] = value
        return value

    lax.fori_loop(0, BX - 1, backward, zero, unroll=True)


def fetches(sources, targets, sem):
    copies = [
        pltpu.make_async_copy(source, target, sem.at[number])
        for number, (source, target) in enumerate(zip(sources, targets))
    ]
    for copy in copies:
        copy.start()
    return copies


def shapes_of(arrays):
    return [pltpu.VMEM(array.shape, array.dtype) for array in arrays]


def part_copy(source, target, sem, part):
    levels = pl.ds(part * CHUNK, CHUNK)
    pick = lambda ref: ref.at[levels] if len(ref.shape) == 3 else ref.at[:, levels]
    return pltpu.make_async_copy(pick(source), pick(target), sem.at[part])


def coefficients(u, v, w, fluid):
    carried = fluid * 0.125
    mixed = fluid * 0.025
    u_part, v_part, w_part = u * carried, v * carried, w * carried
    return (
        mixed - u_part,
        mixed + u_part,
        mixed - v_part,
        mixed + v_part,
        mixed - w_part,
        mixed + w_part,
    )


def aligned(packed, part, offset):
    return pltpu.roll(packed, lax.rem(offset + 2 * BY - part * CHUNK, BY), axis=1)


def turned_back(value, sub):
    return pltpu.roll(value, BY - sub, axis=1) if sub else value


def merged_sides(south, north, sides, numbers):
    even = lax.rem(lane_index(BX), 2) == 0
    for number in numbers:
        for index in (2 * number, 2 * number + 1):
            sides[index] = jnp.where(
                even,
                pltpu.roll(south[index], 1, axis=1),
                pltpu.roll(north[index], BY - 1, axis=1),
            )


def part_sides(sides, number, part):
    group = part // (PARTS // 2)
    start = 2 * CHUNK * lax.rem(part, PARTS // 2)
    return pltpu.roll(sides[2 * number + group], lax.rem(BY - start, BY), axis=1)


def neighbour_sum(ref, n, level, sub, f, up, down, side, coefs, lane):
    c_east, c_west, c_north, c_south, c_up, c_down = coefs
    f_west = ref[n, level, 7 : 7 + BX]
    f_east = ref[n, level, 9 : 9 + BX]
    side = turned_back(side, 2 * sub)
    f_north = jnp.where(lane == BY - 1, side, pltpu.roll(f, BY - 1, axis=1))
    f_south = jnp.where(lane == 0, side, pltpu.roll(f, 1, axis=1))
    return (
        (c_east * f_east + c_west * f_west)
        + (c_north * f_north + c_south * f_south)
        + (c_up * up + c_down * down)
    )


def put_rows(fields, west, east, numbers):
    for slot, number in enumerate(numbers):
        rows = fields.at[slot].reshape(NZ * ROWS, BY)
        rows[pl.ds(7, NZ, stride=ROWS), :] = west[number * NZ : (number + 1) * NZ, :]
        rows[pl.ds(8 + BX, NZ, stride=ROWS), :] = east[number * NZ : (number + 1) * NZ, :]


def near_levels(level, sub):
    below = jnp.maximum(level - 1, 0) if sub == 0 else level - 1
    above = jnp.minimum(level + 1, NZ - 1) if sub == CHUNK - 1 else level + 1
    return below, above


def source_kernel(*refs):
    fields_hbm, wall_hbm = refs[:2]
    inputs, refs = refs[2:13], refs[13:]
    new_hbm, waves_hbm, condensed_hbm = refs[:3]
    held, refs = refs[3:14], refs[14:]
    heights, west, east, south, north = held[:5]
    vertical, vertical_right, to_waves, edge_rows, edges, factors = held[5:]
    fields, wall, new, source, waves, reduced, condensed, sides = refs[:8]
    in_sem, wall_sem, out_sem, held_sem, last_sem = refs[8:]
    copies = fetches(inputs[:5], held[:5], held_sem)

    def field_copy(part):
        levels = pl.ds(part * CHUNK, CHUNK)
        return pltpu.make_async_copy(
            fields_hbm.at[pl.ds(0, 3), levels],
            fields.at[:, levels, pl.ds(8, BX)],
            in_sem.at[part],
        )

    for part in range(PARTS):
        field_copy(part).start()
        part_copy(wall_hbm, wall, wall_sem, part).start()
    tables = fetches(inputs[5:], held[5:], held_sem.at[pl.ds(5, 6)])
    for copy in copies:
        copy.wait()
    put_rows(fields, west, east, range(3))
    merged_sides(south, north, sides, range(3))
    field_copy(0).wait()

    lane = lane_index(BX)
    row = row_index(BX)
    zero = jnp.zeros((BX, BY), f32)

    def part_step(part, carry):
        @pl.when(part < PARTS - 1)
        def _():
            field_copy(part + 1).wait()

        part_copy(wall_hbm, wall, wall_sem, part).wait()
        w_below, v_edge = carry
        turned = [part_sides(sides, n, part) for n in range(3)]
        ends = zero
        for sub in range(CHUNK):
            level = part * CHUNK + sub
            below, above = near_levels(level, sub)
            u, v, w = [fields[n, level, 8 : 8 + BX] for n in range(3)]
            fluid = jnp.where(level >= heights[...], 1.0, 0.0).astype(f32)
            coefs = coefficients(u, v, w, fluid)
            speed = jnp.sqrt(u * u + v * v + w * w + 0.01)
            own = fluid * (0.85 - 0.2 * wall[level].astype(f32) * speed)
            results = []
            for n, f in enumerate((u, v, w)):
                total = own * f + neighbour_sum(
                    fields,
                    n,
                    level,
                    sub,
                    f,
                    fields[n, above, 8 : 8 + BX],
                    fields[n, below, 8 : 8 + BX],
                    turned[n],
                    coefs,
                    lane,
                )
                new[n, level] = total
                results.append(total)
            u_new, v_new, w_new = results
            u_behind = jnp.where(row == 0, 0.0, pltpu.roll(u_new, 1, axis=0))
            v_behind = pltpu.roll(v_new, 1, axis=1)
            ends = jnp.where(lane == sub, turned_back(v_behind, BY - sub), ends)
            v_behind = jnp.where(lane == 0, 0.0, v_behind)
            divergence = (u_new - u_behind) + (v_new - v_behind) + (w_new - w_below)
            source[pl.ds(level, BX, stride=NZ), :] = -4.0 * divergence
            source[pl.ds(BX * NZ + level, 1), :] = 4.0 * u_new[BX - 1 :]
            w_below = w_new
        v_edge = v_edge + pltpu.roll(ends, part * CHUNK, axis=1)
        part_copy(new, new_hbm, out_sem, part).start()
        return w_below, v_edge

    _, v_edge = lax.fori_loop(0, PARTS, part_step, (zero, zero))

    for copy in tables:
        copy.wait()
    for i in range(1, BX):
        along_y = times_right(source[i * NZ : (i + 1) * NZ, :], to_waves[...])
        waves[i - 1] = times_left(vertical[...], along_y)
    own_x = times_left(vertical[...], source[0:NZ, :])
    next_x = times_left(vertical[...], source[BX * NZ : (BX + 1) * NZ, :])

    waves_copy = pltpu.make_async_copy(waves, waves_hbm, last_sem.at[0])
    waves_copy.start()
    eliminate(waves, factors, reduced)

    own_x = own_x + times_right(reduced[0], edge_rows[...])
    next_x = next_x + times_right(reduced[BX - 2], edge_rows[...])
    lane_z = lane_index(NZ)
    next_y = times_right(4.0 * v_edge[:, :NZ], vertical_right[...])
    packed = jnp.concatenate([zero[:, :NZ], next_y, jnp.zeros((2 * BX, NZ), f32)], axis=0).T
    for i in range(1, BX):
        merged = jnp.where(lane_z == 0, waves[i - 1], reduced[i - 1])
        ends = pltpu.roll(times_right(merged, edges[...]), i, axis=1)
        packed = packed + jnp.where((lane_z == i) | (lane_z == BX + i), ends, 0.0)
    condensed[pl.ds(0, NZ, stride=4), :] = own_x
    condensed[pl.ds(1, NZ, stride=4), :] = next_x
    condensed[pl.ds(2, NZ, stride=4), :] = packed
    condensed[pl.ds(3, NZ, stride=4), :] = jnp.zeros((NZ, BY), f32)
    condensed[4 * NZ :, :] = jnp.zeros((4 * (ND - NZ), BY), f32)
    condensed_copy = pltpu.make_async_copy(condensed, condensed_hbm, last_sem.at[1])
    condensed_copy.start()
    waves_copy.wait()
    condensed_copy.wait()
    for part in range(PARTS):
        part_copy(new, new_hbm, out_sem, part).wait()


vmem_spec = pl.BlockSpec(memory_space=pltpu.VMEM)
any_spec = pl.BlockSpec(memory_space=pl.ANY)


def condensed_source(fields, wall_class, heights, west, east, south, north, tables):
    names = ("vertical", "vertical_right", "to_waves", "edge_rows", "edges", "factors")
    held = [heights, west, east, south, north] + [tables[name] for name in names]
    return pl.pallas_call(
        source_kernel,
        in_specs=[any_spec] * 13,
        out_specs=[any_spec] * 3,
        out_shape=[
            jax.ShapeDtypeStruct((3, NZ, BX, BY), f32),
            jax.ShapeDtypeStruct((BX - 1, NZ, BY), f32),
            jax.ShapeDtypeStruct((4 * ND, BY), f32),
        ],
        scratch_shapes=shapes_of(held)
        + [
            pltpu.VMEM((3, NZ, ROWS, BY), f32),
            pltpu.VMEM((NZ, BX, BY), jnp.int32),
            pltpu.VMEM((3, NZ, BX, BY), f32),
            pltpu.VMEM(((BX + 1) * NZ, BY), f32),
            pltpu.VMEM((BX - 1, NZ, BY), f32),
            pltpu.VMEM((BX - 1, NZ, BY), f32),
            pltpu.VMEM((4 * ND, BY), f32),
            pltpu.VMEM((10, BX, BY), f32),
            pltpu.SemaphoreType.DMA((PARTS,)),
            pltpu.SemaphoreType.DMA((PARTS,)),
            pltpu.SemaphoreType.DMA((PARTS,)),
            pltpu.SemaphoreType.DMA((11,)),
            pltpu.SemaphoreType.DMA((2,)),
        ],
        compiler_params=pltpu.CompilerParams(vmem_limit_bytes=GRANT),
        cost_estimate=pl.CostEstimate(flops=0, bytes_accessed=40000000, transcendentals=0),
    )(fields, wall_class, *held)


def scalar_kernel(*refs):
    fields_hbm, wall_hbm = refs[:2]
    inputs, new_hbm, held, refs = refs[2:7], refs[7], refs[8:13], refs[13:]
    heights, west, east, south, north = held
    fields, scalars, wall, new, sides = refs[:5]
    in_sem, scalar_sem, wall_sem, out_sem, held_sem = refs[5:]
    copies = fetches(inputs, held, held_sem)

    def out_copy(part):
        levels = pl.ds(part * CHUNK, CHUNK)
        return pltpu.make_async_copy(
            new.at[:, levels], new_hbm.at[pl.ds(3, 2), levels], out_sem.at[part]
        )

    def in_copy(part):
        levels = pl.ds(part * CHUNK, CHUNK)
        return pltpu.make_async_copy(
            fields_hbm.at[pl.ds(0, 3), levels], fields.at[:, levels], in_sem.at[part]
        )

    def scalar_copy(part):
        levels = pl.ds(part * CHUNK, CHUNK)
        return pltpu.make_async_copy(
            fields_hbm.at[pl.ds(3, 2), levels],
            scalars.at[:, levels, pl.ds(8, BX)],
            scalar_sem.at[part],
        )

    for part in range(PARTS):
        in_copy(part).start()
        scalar_copy(part).start()
        part_copy(wall_hbm, wall, wall_sem, part).start()
    for copy in copies:
        copy.wait()
    put_rows(scalars, west, east, (3, 4))
    merged_sides(south, north, sides, (3, 4))
    scalar_copy(0).wait()
    lane = lane_index(BX)

    def part_step(part, carry):
        @pl.when(part < PARTS - 1)
        def _():
            scalar_copy(part + 1).wait()

        in_copy(part).wait()
        part_copy(wall_hbm, wall, wall_sem, part).wait()
        turned = [part_sides(sides, 3 + n, part) for n in range(2)]
        for sub in range(CHUNK):
            level = part * CHUNK + sub
            below, above = near_levels(level, sub)
            fluid = jnp.where(level >= heights[...], 1.0, 0.0).astype(f32)
            coefs = coefficients(fields[0, level], fields[1, level], fields[2, level], fluid)
            flux = fluid * (0.15 * wall[level].astype(f32))
            own = 1.0 - fluid * 0.15 - flux
            for n, target in enumerate((1.0, -0.5)):
                f = scalars[n, level, 8 : 8 + BX]
                new[n, level] = (own * f + target * flux) + neighbour_sum(
                    scalars,
                    n,
                    level,
                    sub,
                    f,
                    scalars[n, above, 8 : 8 + BX],
                    scalars[n, below, 8 : 8 + BX],
                    turned[n],
                    coefs,
                    lane,
                )
        out_copy(part).start()
        return carry

    lax.fori_loop(0, PARTS, part_step, 0)
    for part in range(PARTS):
        out_copy(part).wait()


def new_scalars(fields, wall_class, *held):
    return pl.pallas_call(
        scalar_kernel,
        in_specs=[any_spec] * 7,
        out_specs=any_spec,
        out_shape=jax.ShapeDtypeStruct((5, NZ, BX, BY), f32),
        scratch_shapes=shapes_of(held)
        + [
            pltpu.VMEM((3, NZ, BX, BY), f32),
            pltpu.VMEM((2, NZ, ROWS, BY), f32),
            pltpu.VMEM((NZ, BX, BY), jnp.int32),
            pltpu.VMEM((2, NZ, BX, BY), f32),
            pltpu.VMEM((10, BX, BY), f32),
            pltpu.SemaphoreType.DMA((PARTS,)),
            pltpu.SemaphoreType.DMA((PARTS,)),
            pltpu.SemaphoreType.DMA((PARTS,)),
            pltpu.SemaphoreType.DMA((PARTS,)),
            pltpu.SemaphoreType.DMA((5,)),
        ],
        compiler_params=pltpu.CompilerParams(vmem_limit_bytes=GRANT),
        cost_estimate=pl.CostEstimate(flops=0, bytes_accessed=30000000, transcendentals=0),
    )(fields, wall_class, *held)


def blockwise(values, stacks):
    parts = []
    for b in range(RY):
        other = (-b) % RY
        pair = jnp.concatenate(
            [values[b * CX : (b + 1) * CX], values[other * CX : (other + 1) * CX]], axis=1
        )
        out = dot(jnp.concatenate(split(pair), axis=0), stacks[b])
        parts.append(out[:CX, :BY] + out[:CX, BY:] + out[CX:, :BY])
    return jnp.concatenate(parts, axis=0)


def per_column(values, mirrored, table):
    pair = values + pltpu.roll(mirrored, BX, axis=1)
    pair = pair + pltpu.roll(pair, 2 * BX, axis=1)
    lane, row = lane_index(ND), row_index(ND)
    mine = lax.rem(row, CX)
    wide = jnp.concatenate(
        [jnp.where(mine == 2 * q + lane // 64, pair, 0.0) for q in range(CX // 2)], axis=1
    )
    out = dot(jnp.concatenate(split(wide), axis=0), table)
    top, bottom = out[:ND], out[ND:]
    out = top + pltpu.roll(top, BY - BX, axis=1) + bottom
    return jnp.where(lane < BX, out, 0.0)


skeleton_names = (
    "grid",
    "mirrored",
    "y_forward",
    "x_forward",
    "eigen_x",
    "eigen_y",
    "swap",
    "y_inverse",
    "x_inverse",
    "grid_back",
)


def skeleton_kernel(mode_eigen, *refs):
    inputs, answer_hbm, held, refs = refs[:11], refs[11], refs[12:23], refs[23:]
    received, grid, mirrored, y_forward, x_forward, eigen_x, eigen_y = held[:7]
    swap, y_inverse, x_inverse, grid_back = held[7:]
    answer, held_sem, last_sem = refs
    copies = fetches(inputs, held, held_sem)
    def wait(first, last):
        for copy in copies[first:last]:
            copy.wait()

    wait(0, 3)
    own_x = received[pl.ds(0, ND, stride=4), :]
    next_x = received[pl.ds(1, ND, stride=4), :]
    lines_y = received[pl.ds(2, ND, stride=4), :]
    lane = lane_index(ND)
    lines_x = own_x + pltpu.roll(next_x, RY, axis=0)
    before = pltpu.roll(lines_y, BY - BX, axis=1).reshape(CX, RY, BY)
    before = pltpu.roll(before, 1, axis=1).reshape(ND, BY)
    lines_y = jnp.where(lane < BX, lines_y + before, 0.0)

    both = times_left(grid[...], jnp.concatenate([lines_x, lines_y], axis=1))
    turned = times_left(mirrored[...], lines_y)
    wait(3, 4)
    spec_x = blockwise(both[:, :BY], y_forward).T
    wait(4, 7)
    spec_y = per_column(both[:, BY:], turned, x_forward[...]).T

    base = eigen_y[...] + mode_eigen[0]
    total_x = jnp.zeros((BY, ND), f32)
    sums = []
    for a in range(BX):
        value = (spec_x + spec_y[a : a + 1]) / (base + eigen_x[a : a + 1])
        total_x = total_x + value
        sums.append(jnp.sum(value, axis=0, keepdims=True))
    total_y = jnp.concatenate(sums, axis=0)
    high, low = split(total_y)
    wait(7, 11)
    turned = dot(high, swap[...]) + dot(low, swap[...])
    fill = jnp.zeros((ND - BX, ND), f32)
    total_y = jnp.concatenate([total_y, fill], axis=0).T
    turned = jnp.concatenate([turned, fill], axis=0).T
    lines_x = blockwise(total_x.T, y_inverse)
    lines_y = per_column(total_y, turned, x_inverse[...])
    both = times_left(grid_back[...], jnp.concatenate([lines_x, lines_y], axis=1))
    own_x, own_y = both[:, :BY], both[:, BY:]
    next_x = pltpu.roll(own_x, ND - RY, axis=0)
    next_y = pltpu.roll(own_y.reshape(CX, RY, BY), RY - 1, axis=1).reshape(ND, BY)
    answer[pl.ds(0, ND, stride=4), :] = own_x
    answer[pl.ds(1, ND, stride=4), :] = next_x
    answer[pl.ds(2, ND, stride=4), :] = own_y + pltpu.roll(next_y, BX, axis=1)
    answer[pl.ds(3, ND, stride=4), :] = jnp.zeros((ND, BY), f32)
    answer_copy = pltpu.make_async_copy(answer, answer_hbm, last_sem.at[0])
    answer_copy.start()
    answer_copy.wait()


def skeleton_solve(received, mode_eigen, tables):
    held = [received] + [tables[name] for name in skeleton_names]
    return pl.pallas_call(
        skeleton_kernel,
        in_specs=[pl.BlockSpec(memory_space=pltpu.SMEM)] + [any_spec] * 11,
        out_specs=any_spec,
        out_shape=jax.ShapeDtypeStruct((4 * ND, BY), f32),
        scratch_shapes=shapes_of(held)
        + [
            pltpu.VMEM((4 * ND, BY), f32),
            pltpu.SemaphoreType.DMA((11,)),
            pltpu.SemaphoreType.DMA((1,)),
        ],
        compiler_params=pltpu.CompilerParams(vmem_limit_bytes=GRANT),
    )(mode_eigen, *held)


correct_names = (
    "factors",
    "plain_sines",
    "near_far",
    "vertical",
    "vertical_right",
    "from_waves",
)


def correct_kernel(*refs):
    before_hbm, inputs = refs[0], refs[1:10]
    new_hbm, pressure_hbm, held, refs = refs[11], refs[12], refs[13:22], refs[22:]
    answer, waves, factors, plain_sines, near_far = held[:5]
    vertical, vertical_right, from_waves, heights = held[5:]
    velocity, pressure, reduced, in_sem, out_sem, pressure_sem, held_sem = refs
    copies = fetches(inputs, held, held_sem)

    def pressure_copy(part):
        levels = pl.ds(part * CHUNK, CHUNK)
        return pltpu.make_async_copy(
            pressure.at[levels, pl.ds(0, BX)], pressure_hbm.at[levels], pressure_sem.at[part]
        )

    def out_copy(part):
        levels = pl.ds(part * CHUNK, CHUNK)
        return pltpu.make_async_copy(
            velocity.at[:, levels], new_hbm.at[pl.ds(0, 3), levels], out_sem.at[part]
        )

    for copy in copies[:5]:
        copy.wait()
    for part in range(PARTS):
        part_copy(before_hbm, velocity, in_sem, part).start()
    own_x = answer[pl.ds(0, NZ, stride=4), :]
    next_x = answer[pl.ds(1, NZ, stride=4), :]
    lines_y = answer[pl.ds(2, NZ, stride=4), :]
    lane_z = lane_index(NZ)
    near, far = near_far[0:1], near_far[1:2]
    for i in range(1, BX):
        rhs = waves[i - 1] + lines_y[:, i : i + 1] * near + lines_y[:, BX + i : BX + i + 1] * far
        if i == 1:
            rhs = rhs + times_right(own_x, plain_sines[...])
        if i == BX - 1:
            rhs = rhs + times_right(next_x, plain_sines[...])
        reduced[i - 1] = rhs
    eliminate(reduced, factors, reduced)

    for copy in copies[5:]:
        copy.wait()
    rows = pressure.reshape(NZ * TALL, BY)
    rows[pl.ds(0, NZ, stride=TALL), :] = times_left(vertical[...], own_x)
    rows[pl.ds(BX, NZ, stride=TALL), :] = times_left(vertical[...], next_x)
    for i in range(1, BX):
        merged = jnp.where(lane_z == 0, lines_y[:, i : i + 1], reduced[i - 1])
        along_y = times_right(merged, from_waves[...])
        rows[pl.ds(i, NZ, stride=TALL), :] = times_left(vertical[...], along_y)
    tall = jnp.concatenate([lines_y, jnp.zeros((BY - NZ, BY), f32)], axis=0).T
    north = times_right(tall[BX : 2 * BX, :NZ], vertical_right[...])
    north = jnp.concatenate([north, jnp.zeros((BX, BY - NZ), f32)], axis=1)

    lane = lane_index(BX)

    def part_step(part, here):
        part_copy(before_hbm, velocity, in_sem, part).wait()
        sides = aligned(north, part, BY - 1)
        for sub in range(CHUNK):
            level = part * CHUNK + sub
            _, above_level = near_levels(level, sub)
            above = pressure[above_level, 0:BX]
            if sub == CHUNK - 1:
                above = jnp.where(level == NZ - 1, -here, above)
            east = pressure[level, 1 : BX + 1]
            side = jnp.where(
                lane == BY - 1, turned_back(sides, sub), pltpu.roll(here, BY - 1, axis=1)
            )
            factor = jnp.where(level >= heights[...], 0.25, 0.0).astype(f32)
            velocity[0, level] = velocity[0, level] - factor * (east - here)
            velocity[1, level] = velocity[1, level] - factor * (side - here)
            velocity[2, level] = velocity[2, level] - factor * (above - here)
            here = above
        out_copy(part).start()
        pressure_copy(part).start()
        return here

    lax.fori_loop(0, PARTS, part_step, pressure[0, 0:BX])
    for part in range(PARTS):
        out_copy(part).wait()
        pressure_copy(part).wait()


def corrected(before, waves, answer, heights, scalars, tables):
    held = [answer, waves] + [tables[name] for name in correct_names] + [heights]
    return pl.pallas_call(
        correct_kernel,
        in_specs=[any_spec] * 11,
        out_specs=[any_spec, any_spec],
        out_shape=[
            jax.ShapeDtypeStruct((5, NZ, BX, BY), f32),
            jax.ShapeDtypeStruct((NZ, BX, BY), f32),
        ],
        scratch_shapes=shapes_of(held)
        + [
            pltpu.VMEM((3, NZ, BX, BY), f32),
            pltpu.VMEM((NZ, TALL, BY), f32),
            pltpu.VMEM((BX - 1, NZ, BY), f32),
            pltpu.SemaphoreType.DMA((PARTS,)),
            pltpu.SemaphoreType.DMA((PARTS,)),
            pltpu.SemaphoreType.DMA((PARTS,)),
            pltpu.SemaphoreType.DMA((9,)),
        ],
        input_output_aliases={10: 0},
        compiler_params=pltpu.CompilerParams(vmem_limit_bytes=GRANT),
    )(before, *held, scalars)


def ring(value, axis, step):
    count = lax.axis_size(axis)
    return lax.ppermute(value, axis, [(n, (n + step) % count) for n in range(count)])


def exchanged(value):
    value = value.reshape(ND, 4, BY)
    return lax.all_to_all(value, ("col", "row"), 0, 0, tiled=True).reshape(4 * ND, BY)


def on_device(fields, heights, wall_class):
    block = {name: jnp.asarray(table) for name, table in block_tables().items()}
    skeleton = {name: jnp.asarray(table) for name, table in skeleton_tables().items()}
    first_x, last_x, first_y, last_y = block_edges(fields)
    west = ring(last_x, "col", 1)
    east = ring(first_x, "col", -1)
    south = ring(last_y, "row", 1)
    north = ring(first_y, "row", -1)
    before, waves, condensed = condensed_source(
        fields, wall_class, heights, west, east, south, north, block
    )
    received = exchanged(condensed)
    scalars = new_scalars(fields, wall_class, heights, west, east, south, north)
    mode = lax.axis_index("col") * RY + lax.axis_index("row")
    eigen = 2.0 - 2.0 * np.cos(np.pi * (np.arange(ND) + 0.5) / NZ)
    eigen[NZ:] = 1.0
    mode_eigen = lax.dynamic_slice(jnp.asarray(eigen.astype(np.float32)), (mode,), (1,))
    solved = skeleton_solve(received, mode_eigen, skeleton)
    answer = exchanged(solved)
    return tuple(corrected(before, waves, answer, heights, scalars, block))


def solution(mesh):
    in_specs = (P(None, None, "col", "row"), P("col", "row"), P(None, "col", "row"))
    out_specs = (P(None, None, "col", "row"), P(None, "col", "row"))
    return jax.shard_map(
        on_device, mesh=mesh, in_specs=in_specs, out_specs=out_specs, check_vma=False
    )
```

```python
import functools
import math

import jax
import jax.numpy as jnp
import ml_dtypes
import numpy as np
from jax import lax
from jax.experimental import pallas as pl
from jax.experimental.pallas import tpu as pltpu
from jax.sharding import PartitionSpec as P

NZ, BX, BY = 96, 32, 128
CX, RY = 16, 8
ND = CX * RY
CHUNK = 8
ROWS = BX + 16
TALL = BX + 8
PARTS = NZ // CHUNK
bf16 = jnp.bfloat16
f32 = jnp.float32
GRANT = 64 * 1024 * 1024


def halves(matrix):
    high = matrix.astype(ml_dtypes.bfloat16)
    low = (matrix - high.astype(np.float64)).astype(ml_dtypes.bfloat16)
    return high, low


def right_stack(matrix):
    high, low = halves(matrix)
    return np.block([[high, low], [high, np.zeros_like(low)]])


def left_stack(matrix):
    high, low = halves(matrix)
    return np.block([[high, high], [low, np.zeros_like(low)]])


def wide_stack(matrix):
    high, low = halves(matrix)
    return np.concatenate([high, low], axis=1)


def cas(angle):
    return np.cos(angle) + np.sin(angle)


def block_tables():
    levels = np.arange(NZ) + 0.5
    vertical = np.sqrt(2.0 / NZ) * np.cos(np.pi * np.outer(levels, levels) / NZ)
    waves = np.arange(BY)
    sines = np.sin(np.pi * np.outer(waves, waves) / BY)
    to_waves = sines.copy()
    to_waves[0, 0] = 1.0
    from_waves = sines * (2.0 / BY)
    edge_rows = from_waves.copy()
    from_waves[0, 0] = 1.0
    diagonal = (
        2.0
        + (2.0 - 2.0 * np.cos(np.pi * levels / NZ))[:, None]
        + (2.0 - 2.0 * np.cos(np.pi * waves / BY))[None, :]
    )
    factors = [np.zeros((NZ, BY))]
    for _ in range(1, BX):
        factors.append(1.0 / (diagonal - factors[-1]))
    edges = np.zeros((BY, BY))
    edges[:, 0] = edge_rows[:, 1]
    edges[0, 0] = 1.0
    edges[:, BX] = edge_rows[:, BY - 1]
    near = sines[1].copy()
    far = sines[BY - 1].copy()
    return dict(
        vertical=left_stack(vertical),
        vertical_right=right_stack(vertical),
        to_waves=right_stack(-4.0 * to_waves),
        plain_sines=right_stack(sines),
        edge_rows=right_stack(edge_rows),
        from_waves=right_stack(from_waves),
        edges=right_stack(edges),
        factors=np.stack(factors[1:]).astype(np.float32),
        near_far=np.stack([near, far] + [np.zeros(BY)] * 6).astype(np.float32),
    )


def skeleton_tables():
    total_x, total_y = CX * BX, RY * BY
    grid = np.zeros((RY, CX, CX, RY))
    a0, c = np.arange(CX), np.arange(CX)
    b0, r = np.arange(RY), np.arange(RY)
    part_x = cas(2 * np.pi * np.outer(a0, c) / CX)
    part_y = cas(2 * np.pi * np.outer(b0, r) / RY)
    grid = np.einsum("ac,br->bacr", part_x, part_y)
    mirrored = grid[:, -a0 % CX]
    grid = grid.reshape(ND, ND)
    mirrored = mirrored.reshape(ND, ND)
    j, i = np.arange(BY), np.arange(BX)
    b1, a1 = np.arange(BY), np.arange(BX)
    y_forward, y_inverse = [], []
    for b in range(RY):
        angle = 2 * np.pi * np.outer(j, b + RY * b1) / total_y
        y_forward.append(np.concatenate([np.cos(angle), np.sin(angle)]))
        angle_other = 2 * np.pi * np.outer(j, (-b) % RY + RY * b1) / total_y
        y_inverse.append(np.concatenate([np.cos(angle).T, np.sin(angle_other).T]))
    x_forward, x_inverse = [], []
    for a in range(CX):
        angle = 2 * np.pi * np.outer(i, a + CX * a1) / total_x
        x_forward.append(np.concatenate([np.cos(angle), np.sin(angle)]))
        angle_other = 2 * np.pi * np.outer(i, (-a) % CX + CX * a1) / total_x
        x_inverse.append(np.concatenate([np.cos(angle).T, np.sin(angle_other).T]))

    def lanes(blocks):
        matrix = np.concatenate(blocks)
        out = np.concatenate(halves(matrix), axis=1)
        return np.concatenate([out, np.zeros((out.shape[0], 64), out.dtype)], axis=1)

    lane = np.arange(ND)
    lane_b0, lane_a0 = lane // CX, lane % CX
    wave_x = lane_a0[None, :] + CX * a1[:, None]
    wave_y = lane_b0[None, :] + RY * b1[:, None]
    swap = np.zeros((ND, ND))
    swap[(lane_b0 * CX + (-lane_a0) % CX), lane] = 1.0
    return dict(
        grid=left_stack(grid),
        mirrored=left_stack(mirrored),
        grid_back=left_stack(grid.T / (total_x * total_y)),
        y_forward=np.stack([wide_stack(m) for m in y_forward]),
        y_inverse=np.stack([wide_stack(m) for m in y_inverse]),
        x_forward=lanes(x_forward),
        x_inverse=lanes(x_inverse),
        swap=swap.astype(ml_dtypes.bfloat16),
        eigen_x=(2 - 2 * np.cos(2 * np.pi * wave_x / total_x)).astype(np.float32),
        eigen_y=(2 - 2 * np.cos(2 * np.pi * wave_y / total_y)).astype(np.float32),
    )


def split(values):
    high = values.astype(bf16)
    return high, (values - high.astype(f32)).astype(bf16)


def dot(left, right):
    return jnp.dot(left, right, preferred_element_type=f32)


def times_right(values, stack):
    out = dot(jnp.concatenate(split(values), axis=1), stack)
    half = out.shape[1] // 2
    return out[:, :half] + out[:, half:]


def times_left(stack, values):
    out = dot(stack, jnp.concatenate(split(values), axis=0))
    half = out.shape[0] // 2
    return out[:half] + out[half:]


def lane_index(rows):
    return lax.broadcasted_iota(jnp.int32, (rows, BY), 1)


def row_index(rows):
    return lax.broadcasted_iota(jnp.int32, (rows, BY), 0)


def edge_kernel(fields, first_x, last_x, first_y, last_y, held, west, east, south, north, *sems):
    sem, out_sem = sems

    def copy(number):
        return pltpu.make_async_copy(fields.at[number], held.at[number], sem.at[number])

    for number in range(5):
        copy(number).start()
    lane = lane_index(BX)

    def step(number, carry):
        copy(number).wait()
        rows = held.at[number].reshape(NZ * BX, BY)
        east[pl.ds(pl.multiple_of(number * NZ, NZ), NZ), :] = rows[pl.ds(0, NZ, stride=BX), :]
        west[pl.ds(pl.multiple_of(number * NZ, NZ), NZ), :] = rows[pl.ds(BX - 1, NZ, stride=BX), :]
        for group in range(2):
            first, last = jnp.zeros((BX, BY), f32), jnp.zeros((BX, BY), f32)
            for level in range(NZ // 2):
                turned = held[number, group * (NZ // 2) + level]
                if level:
                    turned = pltpu.roll(turned, 2 * level, axis=1)
                first = jnp.where(lane == 2 * level, turned, first)
                last = jnp.where(lane == (2 * level - 1) % BY, turned, last)
            north[2 * number + group] = first
            south[2 * number + group] = last
        return carry

    lax.fori_loop(0, 5, step, 0)
    for copied in fetches(
        [east, west, north, south], [first_x, last_x, first_y, last_y], out_sem
    ):
        copied.wait()


def block_edges(fields):
    plane = (5 * NZ, BY)
    packed = (10, BX, BY)
    shapes = [plane, plane, packed, packed]
    return pl.pallas_call(
        edge_kernel,
        in_specs=[any_spec],
        out_specs=[any_spec] * 4,
        out_shape=[jax.ShapeDtypeStruct(shape, f32) for shape in shapes],
        scratch_shapes=[pltpu.VMEM((5, NZ, BX, BY), f32)]
        + [pltpu.VMEM(shape, f32) for shape in shapes]
        + [pltpu.SemaphoreType.DMA((5,)), pltpu.SemaphoreType.DMA((4,))],
        compiler_params=pltpu.CompilerParams(vmem_limit_bytes=GRANT),
    )(fields)


def eliminate(rhs, factors, reduced):
    def forward(index, reduced_prev):
        value = factors[index] * (rhs[index] + reduced_prev)
        reduced[index] = value
        return value

    zero = jnp.zeros((NZ, BY), f32)
    lax.fori_loop(0, BX - 1, forward, zero, unroll=True)

    def backward(step, above):
        index = BX - 2 - step
        value = reduced[index] + factors[index] * above
        reduced[index] = value
        return value

    lax.fori_loop(0, BX - 1, backward, zero, unroll=True)


def fetches(sources, targets, sem):
    copies = [
        pltpu.make_async_copy(source, target, sem.at[number])
        for number, (source, target) in enumerate(zip(sources, targets))
    ]
    for copy in copies:
        copy.start()
    return copies


def shapes_of(arrays):
    return [pltpu.VMEM(array.shape, array.dtype) for array in arrays]


def part_copy(source, target, sem, part):
    levels = pl.ds(part * CHUNK, CHUNK)
    pick = lambda ref: ref.at[levels] if len(ref.shape) == 3 else ref.at[:, levels]
    return pltpu.make_async_copy(pick(source), pick(target), sem.at[part])


def coefficients(u, v, w, fluid):
    carried = fluid * 0.125
    mixed = fluid * 0.025
    u_part, v_part, w_part = u * carried, v * carried, w * carried
    return (
        mixed - u_part,
        mixed + u_part,
        mixed - v_part,
        mixed + v_part,
        mixed - w_part,
        mixed + w_part,
    )


def aligned(packed, part, offset):
    return pltpu.roll(packed, lax.rem(offset + 2 * BY - part * CHUNK, BY), axis=1)


def turned_back(value, sub):
    return pltpu.roll(value, BY - sub, axis=1) if sub else value


def merged_sides(south, north, sides, numbers):
    even = lax.rem(lane_index(BX), 2) == 0
    for number in numbers:
        for index in (2 * number, 2 * number + 1):
            sides[index] = jnp.where(
                even,
                pltpu.roll(south[index], 1, axis=1),
                pltpu.roll(north[index], BY - 1, axis=1),
            )


def part_sides(sides, number, part):
    group = part // (PARTS // 2)
    start = 2 * CHUNK * lax.rem(part, PARTS // 2)
    return pltpu.roll(sides[2 * number + group], lax.rem(BY - start, BY), axis=1)


def neighbour_sum(ref, n, level, sub, f, up, down, side, coefs, lane):
    c_east, c_west, c_north, c_south, c_up, c_down = coefs
    f_west = ref[n, level, 7 : 7 + BX]
    f_east = ref[n, level, 9 : 9 + BX]
    side = turned_back(side, 2 * sub)
    f_north = jnp.where(lane == BY - 1, side, pltpu.roll(f, BY - 1, axis=1))
    f_south = jnp.where(lane == 0, side, pltpu.roll(f, 1, axis=1))
    return (
        (c_east * f_east + c_west * f_west)
        + (c_north * f_north + c_south * f_south)
        + (c_up * up + c_down * down)
    )


def put_rows(fields, west, east, numbers):
    for slot, number in enumerate(numbers):
        rows = fields.at[slot].reshape(NZ * ROWS, BY)
        rows[pl.ds(7, NZ, stride=ROWS), :] = west[number * NZ : (number + 1) * NZ, :]
        rows[pl.ds(8 + BX, NZ, stride=ROWS), :] = east[number * NZ : (number + 1) * NZ, :]


def near_levels(level, sub):
    below = jnp.maximum(level - 1, 0) if sub == 0 else level - 1
    above = jnp.minimum(level + 1, NZ - 1) if sub == CHUNK - 1 else level + 1
    return below, above


def source_kernel(*refs):
    fields_hbm, wall_hbm = refs[:2]
    inputs, refs = refs[2:13], refs[13:]
    new_hbm, waves_hbm, condensed_hbm = refs[:3]
    held, refs = refs[3:14], refs[14:]
    heights, west, east, south, north, to_waves = held[:6]
    vertical, vertical_right, edge_rows, edges, factors = held[6:]
    fields, wall, new, source, waves, reduced, condensed, sides, ends_x = refs[:9]
    in_sem, wall_sem, out_sem, held_sem, last_sem = refs[9:]
    copies = fetches(inputs[:6], held[:6], held_sem)

    def field_copy(part):
        levels = pl.ds(part * CHUNK, CHUNK)
        return pltpu.make_async_copy(
            fields_hbm.at[pl.ds(0, 3), levels],
            fields.at[:, levels, pl.ds(8, BX)],
            in_sem.at[part],
        )

    for part in range(PARTS):
        field_copy(part).start()
        part_copy(wall_hbm, wall, wall_sem, part).start()
    tables = fetches(inputs[6:], held[6:], held_sem.at[pl.ds(6, 5)])
    for copy in copies:
        copy.wait()
    put_rows(fields, west, east, range(3))
    merged_sides(south, north, sides, range(3))
    field_copy(0).wait()

    lane = lane_index(BX)
    row = row_index(BX)
    zero = jnp.zeros((BX, BY), f32)

    def spread(part):
        pieces = []
        ends = zero
        for sub in range(CHUNK):
            level = part * CHUNK + sub
            u, v, w = new[0, level], new[1, level], new[2, level]
            if sub:
                w_below = new[2, level - 1]
            else:
                w_below = jnp.where(part > 0, new[2, jnp.maximum(level - 1, 0)], 0.0)
            u_behind = jnp.where(row == 0, 0.0, pltpu.roll(u, 1, axis=0))
            v_behind = pltpu.roll(v, 1, axis=1)
            ends = jnp.where(lane == sub, turned_back(v_behind, BY - sub), ends)
            v_behind = jnp.where(lane == 0, 0.0, v_behind)
            divergence = (u - u_behind) + (v - v_behind) + (w - w_below)
            ends_x[pl.ds(level, 1), :] = -4.0 * divergence[:1]
            ends_x[pl.ds(NZ + level, 1), :] = 4.0 * u[BX - 1 :]
            pieces.append(divergence)
        along_y = times_right(jnp.concatenate(pieces, axis=0), to_waves[...])
        for sub in range(CHUNK):
            rows = pl.ds(part * CHUNK + sub, BX, stride=NZ)
            source[rows, :] = along_y[sub * BX : (sub + 1) * BX]
        return pltpu.roll(ends, part * CHUNK, axis=1)

    def part_step(part, v_edge):
        @pl.when(part < PARTS - 1)
        def _():
            field_copy(part + 1).wait()

        part_copy(wall_hbm, wall, wall_sem, part).wait()
        v_edge = v_edge + jnp.where(part > 0, spread(jnp.maximum(part - 1, 0)), 0.0)
        turned = [part_sides(sides, n, part) for n in range(3)]
        for sub in range(CHUNK):
            level = part * CHUNK + sub
            below, above = near_levels(level, sub)
            u, v, w = [fields[n, level, 8 : 8 + BX] for n in range(3)]
            fluid = jnp.where(level >= heights[...], 1.0, 0.0).astype(f32)
            coefs = coefficients(u, v, w, fluid)
            speed = jnp.sqrt(u * u + v * v + w * w + 0.01)
            own = fluid * (0.85 - 0.2 * wall[level].astype(f32) * speed)
            for n, f in enumerate((u, v, w)):
                new[n, level] = own * f + neighbour_sum(
                    fields,
                    n,
                    level,
                    sub,
                    f,
                    fields[n, above, 8 : 8 + BX],
                    fields[n, below, 8 : 8 + BX],
                    turned[n],
                    coefs,
                    lane,
                )
        part_copy(new, new_hbm, out_sem, part).start()
        return v_edge

    v_edge = lax.fori_loop(0, PARTS, part_step, zero)

    v_edge = v_edge + spread(PARTS - 1)
    for copy in tables:
        copy.wait()
    for i in range(1, BX - 1, 2):
        pair = [source[n * NZ : (n + 1) * NZ, :] for n in (i, i + 1)]
        out = times_left(vertical[...], jnp.concatenate(pair, axis=1))
        waves[i - 1] = out[:, :BY]
        waves[i] = out[:, BY:]
    waves[BX - 2] = times_left(vertical[...], source[(BX - 1) * NZ : BX * NZ, :])
    pair = jnp.concatenate([ends_x[0:NZ, :], ends_x[NZ : 2 * NZ, :]], axis=1)
    out = times_left(vertical[...], pair)
    own_x, next_x = out[:, :BY], out[:, BY:]

    waves_copy = pltpu.make_async_copy(waves, waves_hbm, last_sem.at[0])
    waves_copy.start()
    eliminate(waves, factors, reduced)

    own_x = own_x + times_right(reduced[0], edge_rows[...])
    next_x = next_x + times_right(reduced[BX - 2], edge_rows[...])
    lane_z = lane_index(NZ)
    next_y = times_right(4.0 * v_edge[:, :NZ], vertical_right[...])
    packed = jnp.concatenate([zero[:, :NZ], next_y, jnp.zeros((2 * BX, NZ), f32)], axis=0).T
    for i in range(1, BX):
        merged = jnp.where(lane_z == 0, waves[i - 1], reduced[i - 1])
        ends = pltpu.roll(times_right(merged, edges[...]), i, axis=1)
        packed = packed + jnp.where((lane_z == i) | (lane_z == BX + i), ends, 0.0)
    condensed[pl.ds(0, NZ, stride=4), :] = own_x
    condensed[pl.ds(1, NZ, stride=4), :] = next_x
    condensed[pl.ds(2, NZ, stride=4), :] = packed
    condensed[pl.ds(3, NZ, stride=4), :] = jnp.zeros((NZ, BY), f32)
    condensed[4 * NZ :, :] = jnp.zeros((4 * (ND - NZ), BY), f32)
    condensed_copy = pltpu.make_async_copy(condensed, condensed_hbm, last_sem.at[1])
    condensed_copy.start()
    waves_copy.wait()
    condensed_copy.wait()
    for part in range(PARTS):
        part_copy(new, new_hbm, out_sem, part).wait()


vmem_spec = pl.BlockSpec(memory_space=pltpu.VMEM)
any_spec = pl.BlockSpec(memory_space=pl.ANY)


def condensed_source(fields, wall_class, heights, west, east, south, north, tables):
    names = ("to_waves", "vertical", "vertical_right", "edge_rows", "edges", "factors")
    held = [heights, west, east, south, north] + [tables[name] for name in names]
    return pl.pallas_call(
        source_kernel,
        in_specs=[any_spec] * 13,
        out_specs=[any_spec] * 3,
        out_shape=[
            jax.ShapeDtypeStruct((3, NZ, BX, BY), f32),
            jax.ShapeDtypeStruct((BX - 1, NZ, BY), f32),
            jax.ShapeDtypeStruct((4 * ND, BY), f32),
        ],
        scratch_shapes=shapes_of(held)
        + [
            pltpu.VMEM((3, NZ, ROWS, BY), f32),
            pltpu.VMEM((NZ, BX, BY), jnp.int32),
            pltpu.VMEM((3, NZ, BX, BY), f32),
            pltpu.VMEM((BX * NZ, BY), f32),
            pltpu.VMEM((BX - 1, NZ, BY), f32),
            pltpu.VMEM((BX - 1, NZ, BY), f32),
            pltpu.VMEM((4 * ND, BY), f32),
            pltpu.VMEM((10, BX, BY), f32),
            pltpu.VMEM((2 * NZ, BY), f32),
            pltpu.SemaphoreType.DMA((PARTS,)),
            pltpu.SemaphoreType.DMA((PARTS,)),
            pltpu.SemaphoreType.DMA((PARTS,)),
            pltpu.SemaphoreType.DMA((11,)),
            pltpu.SemaphoreType.DMA((2,)),
        ],
        compiler_params=pltpu.CompilerParams(vmem_limit_bytes=GRANT),
        cost_estimate=pl.CostEstimate(flops=0, bytes_accessed=40000000, transcendentals=0),
    )(fields, wall_class, *held)


def scalar_kernel(*refs):
    fields_hbm, wall_hbm = refs[:2]
    inputs, new_hbm, held, refs = refs[2:7], refs[7], refs[8:13], refs[13:]
    heights, west, east, south, north = held
    fields, scalars, wall, new, sides = refs[:5]
    in_sem, scalar_sem, wall_sem, out_sem, held_sem = refs[5:]
    copies = fetches(inputs, held, held_sem)

    def out_copy(part):
        levels = pl.ds(part * CHUNK, CHUNK)
        return pltpu.make_async_copy(
            new.at[:, levels], new_hbm.at[pl.ds(3, 2), levels], out_sem.at[part]
        )

    def in_copy(part):
        levels = pl.ds(part * CHUNK, CHUNK)
        return pltpu.make_async_copy(
            fields_hbm.at[pl.ds(0, 3), levels], fields.at[:, levels], in_sem.at[part]
        )

    def scalar_copy(part):
        levels = pl.ds(part * CHUNK, CHUNK)
        return pltpu.make_async_copy(
            fields_hbm.at[pl.ds(3, 2), levels],
            scalars.at[:, levels, pl.ds(8, BX)],
            scalar_sem.at[part],
        )

    for part in range(PARTS):
        in_copy(part).start()
        scalar_copy(part).start()
        part_copy(wall_hbm, wall, wall_sem, part).start()
    for copy in copies:
        copy.wait()
    put_rows(scalars, west, east, (3, 4))
    merged_sides(south, north, sides, (3, 4))
    scalar_copy(0).wait()
    lane = lane_index(BX)

    def part_step(part, carry):
        @pl.when(part < PARTS - 1)
        def _():
            scalar_copy(part + 1).wait()

        in_copy(part).wait()
        part_copy(wall_hbm, wall, wall_sem, part).wait()
        turned = [part_sides(sides, 3 + n, part) for n in range(2)]
        for sub in range(CHUNK):
            level = part * CHUNK + sub
            below, above = near_levels(level, sub)
            fluid = jnp.where(level >= heights[...], 1.0, 0.0).astype(f32)
            coefs = coefficients(fields[0, level], fields[1, level], fields[2, level], fluid)
            flux = fluid * (0.15 * wall[level].astype(f32))
            own = 1.0 - fluid * 0.15 - flux
            for n, target in enumerate((1.0, -0.5)):
                f = scalars[n, level, 8 : 8 + BX]
                new[n, level] = (own * f + target * flux) + neighbour_sum(
                    scalars,
                    n,
                    level,
                    sub,
                    f,
                    scalars[n, above, 8 : 8 + BX],
                    scalars[n, below, 8 : 8 + BX],
                    turned[n],
                    coefs,
                    lane,
                )
        out_copy(part).start()
        return carry

    lax.fori_loop(0, PARTS, part_step, 0)
    for part in range(PARTS):
        out_copy(part).wait()


def new_scalars(fields, wall_class, *held):
    return pl.pallas_call(
        scalar_kernel,
        in_specs=[any_spec] * 7,
        out_specs=any_spec,
        out_shape=jax.ShapeDtypeStruct((5, NZ, BX, BY), f32),
        scratch_shapes=shapes_of(held)
        + [
            pltpu.VMEM((3, NZ, BX, BY), f32),
            pltpu.VMEM((2, NZ, ROWS, BY), f32),
            pltpu.VMEM((NZ, BX, BY), jnp.int32),
            pltpu.VMEM((2, NZ, BX, BY), f32),
            pltpu.VMEM((10, BX, BY), f32),
            pltpu.SemaphoreType.DMA((PARTS,)),
            pltpu.SemaphoreType.DMA((PARTS,)),
            pltpu.SemaphoreType.DMA((PARTS,)),
            pltpu.SemaphoreType.DMA((PARTS,)),
            pltpu.SemaphoreType.DMA((5,)),
        ],
        compiler_params=pltpu.CompilerParams(vmem_limit_bytes=GRANT),
        cost_estimate=pl.CostEstimate(flops=0, bytes_accessed=30000000, transcendentals=0),
    )(fields, wall_class, *held)


def blockwise(values, stacks):
    parts = []
    for b in range(RY):
        other = (-b) % RY
        pair = jnp.concatenate(
            [values[b * CX : (b + 1) * CX], values[other * CX : (other + 1) * CX]], axis=1
        )
        out = dot(jnp.concatenate(split(pair), axis=0), stacks[b])
        parts.append(out[:CX, :BY] + out[:CX, BY:] + out[CX:, :BY])
    return jnp.concatenate(parts, axis=0)


def per_column(values, mirrored, table):
    pair = values + pltpu.roll(mirrored, BX, axis=1)
    pair = pair + pltpu.roll(pair, 2 * BX, axis=1)
    lane, row = lane_index(ND), row_index(ND)
    mine = lax.rem(row, CX)
    wide = jnp.concatenate(
        [jnp.where(mine == 2 * q + lane // 64, pair, 0.0) for q in range(CX // 2)], axis=1
    )
    out = dot(jnp.concatenate(split(wide), axis=0), table)
    top, bottom = out[:ND], out[ND:]
    out = top + pltpu.roll(top, BY - BX, axis=1) + bottom
    return jnp.where(lane < BX, out, 0.0)


skeleton_names = (
    "grid",
    "mirrored",
    "y_forward",
    "x_forward",
    "eigen_x",
    "eigen_y",
    "swap",
    "y_inverse",
    "x_inverse",
    "grid_back",
)


def skeleton_kernel(mode_eigen, *refs):
    inputs, answer_hbm, held, refs = refs[:11], refs[11], refs[12:23], refs[23:]
    received, grid, mirrored, y_forward, x_forward, eigen_x, eigen_y = held[:7]
    swap, y_inverse, x_inverse, grid_back = held[7:]
    answer, held_sem, last_sem = refs
    copies = fetches(inputs, held, held_sem)
    def wait(first, last):
        for copy in copies[first:last]:
            copy.wait()

    wait(0, 3)
    own_x = received[pl.ds(0, ND, stride=4), :]
    next_x = received[pl.ds(1, ND, stride=4), :]
    lines_y = received[pl.ds(2, ND, stride=4), :]
    lane = lane_index(ND)
    lines_x = own_x + pltpu.roll(next_x, RY, axis=0)
    before = pltpu.roll(lines_y, BY - BX, axis=1).reshape(CX, RY, BY)
    before = pltpu.roll(before, 1, axis=1).reshape(ND, BY)
    lines_y = jnp.where(lane < BX, lines_y + before, 0.0)

    both = times_left(grid[...], jnp.concatenate([lines_x, lines_y], axis=1))
    turned = times_left(mirrored[...], lines_y)
    wait(3, 4)
    spec_x = blockwise(both[:, :BY], y_forward).T
    wait(4, 7)
    spec_y = per_column(both[:, BY:], turned, x_forward[...]).T

    base = eigen_y[...] + mode_eigen[0]
    total_x = jnp.zeros((BY, ND), f32)
    sums = []
    for a in range(BX):
        value = (spec_x + spec_y[a : a + 1]) / (base + eigen_x[a : a + 1])
        total_x = total_x + value
        sums.append(jnp.sum(value, axis=0, keepdims=True))
    total_y = jnp.concatenate(sums, axis=0)
    high, low = split(total_y)
    wait(7, 11)
    turned = dot(high, swap[...]) + dot(low, swap[...])
    fill = jnp.zeros((ND - BX, ND), f32)
    total_y = jnp.concatenate([total_y, fill], axis=0).T
    turned = jnp.concatenate([turned, fill], axis=0).T
    lines_x = blockwise(total_x.T, y_inverse)
    lines_y = per_column(total_y, turned, x_inverse[...])
    both = times_left(grid_back[...], jnp.concatenate([lines_x, lines_y], axis=1))
    own_x, own_y = both[:, :BY], both[:, BY:]
    next_x = pltpu.roll(own_x, ND - RY, axis=0)
    next_y = pltpu.roll(own_y.reshape(CX, RY, BY), RY - 1, axis=1).reshape(ND, BY)
    answer[pl.ds(0, ND, stride=4), :] = own_x
    answer[pl.ds(1, ND, stride=4), :] = next_x
    answer[pl.ds(2, ND, stride=4), :] = own_y + pltpu.roll(next_y, BX, axis=1)
    answer[pl.ds(3, ND, stride=4), :] = jnp.zeros((ND, BY), f32)
    answer_copy = pltpu.make_async_copy(answer, answer_hbm, last_sem.at[0])
    answer_copy.start()
    answer_copy.wait()


def skeleton_solve(received, mode_eigen, tables):
    held = [received] + [tables[name] for name in skeleton_names]
    return pl.pallas_call(
        skeleton_kernel,
        in_specs=[pl.BlockSpec(memory_space=pltpu.SMEM)] + [any_spec] * 11,
        out_specs=any_spec,
        out_shape=jax.ShapeDtypeStruct((4 * ND, BY), f32),
        scratch_shapes=shapes_of(held)
        + [
            pltpu.VMEM((4 * ND, BY), f32),
            pltpu.SemaphoreType.DMA((11,)),
            pltpu.SemaphoreType.DMA((1,)),
        ],
        compiler_params=pltpu.CompilerParams(vmem_limit_bytes=GRANT),
    )(mode_eigen, *held)


correct_names = (
    "factors",
    "plain_sines",
    "near_far",
    "vertical",
    "vertical_right",
    "from_waves",
)


def correct_kernel(*refs):
    before_hbm, inputs = refs[0], refs[1:10]
    new_hbm, pressure_hbm, held, refs = refs[11], refs[12], refs[13:22], refs[22:]
    answer, waves, factors, plain_sines, near_far = held[:5]
    vertical, vertical_right, from_waves, heights = held[5:]
    velocity, pressure, reduced, in_sem, out_sem, pressure_sem, held_sem, row_sem = refs
    first = [pl.ds(0, 8), pl.ds(8, 8), pl.ds(16, BX - 17)]
    copies = fetches(inputs[:1], held[:1], held_sem)
    rows_in = []
    for number, rows in enumerate(first):
        pair = [inputs[1].at[rows], inputs[2].at[rows]]
        held_pair = [waves.at[rows], factors.at[rows]]
        rows_in.append(fetches(pair, held_pair, row_sem.at[pl.ds(2 * number, 2)]))
    copies += fetches(inputs[3:], held[3:], held_sem.at[pl.ds(1, 6)])

    def pressure_copy(part):
        levels = pl.ds(part * CHUNK, CHUNK)
        return pltpu.make_async_copy(
            pressure.at[levels, pl.ds(0, BX)], pressure_hbm.at[levels], pressure_sem.at[part]
        )

    def out_copy(part):
        levels = pl.ds(part * CHUNK, CHUNK)
        return pltpu.make_async_copy(
            velocity.at[:, levels], new_hbm.at[pl.ds(0, 3), levels], out_sem.at[part]
        )

    for copy in copies[:3]:
        copy.wait()
    for part in range(PARTS):
        part_copy(before_hbm, velocity, in_sem, part).start()
    own_x = answer[pl.ds(0, NZ, stride=4), :]
    next_x = answer[pl.ds(1, NZ, stride=4), :]
    lines_y = answer[pl.ds(2, NZ, stride=4), :]
    lane_z = lane_index(NZ)
    near, far = near_far[0:1], near_far[1:2]
    for i in range(1, BX):
        if i in (1, 9, 17):
            for copy in rows_in[i // 8]:
                copy.wait()
        rhs = waves[i - 1] + lines_y[:, i : i + 1] * near + lines_y[:, BX + i : BX + i + 1] * far
        if i == 1:
            rhs = rhs + times_right(own_x, plain_sines[...])
        if i == BX - 1:
            rhs = rhs + times_right(next_x, plain_sines[...])
        reduced[i - 1] = rhs
    eliminate(reduced, factors, reduced)

    for copy in copies[3:]:
        copy.wait()
    rows = pressure.reshape(NZ * TALL, BY)
    planes = [own_x]
    for i in range(1, BX):
        merged = jnp.where(lane_z == 0, lines_y[:, i : i + 1], reduced[i - 1])
        planes.append(times_right(merged, from_waves[...]))
        if i % 2:
            out = times_left(vertical[...], jnp.concatenate(planes, axis=1))
            rows[pl.ds(i - 1, NZ, stride=TALL), :] = out[:, :BY]
            rows[pl.ds(i, NZ, stride=TALL), :] = out[:, BY:]
            planes = []
    rows[pl.ds(BX, NZ, stride=TALL), :] = times_left(vertical[...], next_x)
    tall = jnp.concatenate([lines_y, jnp.zeros((BY - NZ, BY), f32)], axis=0).T
    north = times_right(tall[BX : 2 * BX, :NZ], vertical_right[...])
    north = jnp.concatenate([north, jnp.zeros((BX, BY - NZ), f32)], axis=1)

    lane = lane_index(BX)

    def part_step(part, here):
        part_copy(before_hbm, velocity, in_sem, part).wait()
        sides = aligned(north, part, BY - 1)
        for sub in range(CHUNK):
            level = part * CHUNK + sub
            _, above_level = near_levels(level, sub)
            above = pressure[above_level, 0:BX]
            if sub == CHUNK - 1:
                above = jnp.where(level == NZ - 1, -here, above)
            east = pressure[level, 1 : BX + 1]
            side = jnp.where(
                lane == BY - 1, turned_back(sides, sub), pltpu.roll(here, BY - 1, axis=1)
            )
            factor = jnp.where(level >= heights[...], 0.25, 0.0).astype(f32)
            velocity[0, level] = velocity[0, level] - factor * (east - here)
            velocity[1, level] = velocity[1, level] - factor * (side - here)
            velocity[2, level] = velocity[2, level] - factor * (above - here)
            here = above
        out_copy(part).start()
        pressure_copy(part).start()
        return here

    lax.fori_loop(0, PARTS, part_step, pressure[0, 0:BX])
    for part in range(PARTS):
        out_copy(part).wait()
        pressure_copy(part).wait()


def corrected(before, waves, answer, heights, scalars, tables):
    held = [answer, waves] + [tables[name] for name in correct_names] + [heights]
    return pl.pallas_call(
        correct_kernel,
        in_specs=[any_spec] * 11,
        out_specs=[any_spec, any_spec],
        out_shape=[
            jax.ShapeDtypeStruct((5, NZ, BX, BY), f32),
            jax.ShapeDtypeStruct((NZ, BX, BY), f32),
        ],
        scratch_shapes=shapes_of(held)
        + [
            pltpu.VMEM((3, NZ, BX, BY), f32),
            pltpu.VMEM((NZ, TALL, BY), f32),
            pltpu.VMEM((BX - 1, NZ, BY), f32),
            pltpu.SemaphoreType.DMA((PARTS,)),
            pltpu.SemaphoreType.DMA((PARTS,)),
            pltpu.SemaphoreType.DMA((PARTS,)),
            pltpu.SemaphoreType.DMA((7,)),
            pltpu.SemaphoreType.DMA((6,)),
        ],
        input_output_aliases={10: 0},
        compiler_params=pltpu.CompilerParams(vmem_limit_bytes=GRANT),
    )(before, *held, scalars)


def ring(value, axis, step):
    count = lax.axis_size(axis)
    return lax.ppermute(value, axis, [(n, (n + step) % count) for n in range(count)])


def exchanged(value):
    value = value.reshape(ND, 4, BY)
    return lax.all_to_all(value, ("col", "row"), 0, 0, tiled=True).reshape(4 * ND, BY)


def on_device(fields, heights, wall_class):
    block = {name: jnp.asarray(table) for name, table in block_tables().items()}
    skeleton = {name: jnp.asarray(table) for name, table in skeleton_tables().items()}
    first_x, last_x, first_y, last_y = block_edges(fields)
    west = ring(last_x, "col", 1)
    east = ring(first_x, "col", -1)
    south = ring(last_y, "row", 1)
    north = ring(first_y, "row", -1)
    before, waves, condensed = condensed_source(
        fields, wall_class, heights, west, east, south, north, block
    )
    received = exchanged(condensed)
    scalars = new_scalars(fields, wall_class, heights, west, east, south, north)
    mode = lax.axis_index("col") * RY + lax.axis_index("row")
    eigen = 2.0 - 2.0 * np.cos(np.pi * (np.arange(ND) + 0.5) / NZ)
    eigen[NZ:] = 1.0
    mode_eigen = lax.dynamic_slice(jnp.asarray(eigen.astype(np.float32)), (mode,), (1,))
    solved = skeleton_solve(received, mode_eigen, skeleton)
    answer = exchanged(solved)
    return tuple(corrected(before, waves, answer, heights, scalars, block))


def solution(mesh):
    in_specs = (P(None, None, "col", "row"), P("col", "row"), P(None, "col", "row"))
    out_specs = (P(None, None, "col", "row"), P(None, "col", "row"))
    return jax.shard_map(
        on_device, mesh=mesh, in_specs=in_specs, out_specs=out_specs, check_vma=False
    )
```

```python
import functools
import math

import jax
import jax.numpy as jnp
import ml_dtypes
import numpy as np
from jax import lax
from jax.experimental import pallas as pl
from jax.experimental.pallas import tpu as pltpu
from jax.sharding import PartitionSpec as P

NZ, BX, BY = 96, 32, 128
CX, RY = 16, 8
ND = CX * RY
CHUNK = 8
ROWS = BX + 16
TALL = BX + 8
PARTS = NZ // CHUNK
bf16 = jnp.bfloat16
f32 = jnp.float32
GRANT = 64 * 1024 * 1024


def halves(matrix):
    high = matrix.astype(ml_dtypes.bfloat16)
    low = (matrix - high.astype(np.float64)).astype(ml_dtypes.bfloat16)
    return high, low


def right_stack(matrix):
    high, low = halves(matrix)
    return np.block([[high, low], [high, np.zeros_like(low)]])


def left_stack(matrix):
    high, low = halves(matrix)
    return np.block([[high, high], [low, np.zeros_like(low)]])


def wide_stack(matrix):
    high, low = halves(matrix)
    return np.concatenate([high, low], axis=1)


def cas(angle):
    return np.cos(angle) + np.sin(angle)


def block_tables():
    levels = np.arange(NZ) + 0.5
    vertical = np.sqrt(2.0 / NZ) * np.cos(np.pi * np.outer(levels, levels) / NZ)
    waves = np.arange(BY)
    sines = np.sin(np.pi * np.outer(waves, waves) / BY)
    to_waves = sines.copy()
    to_waves[0, 0] = 1.0
    from_waves = sines * (2.0 / BY)
    edge_rows = from_waves.copy()
    from_waves[0, 0] = 1.0
    diagonal = (
        2.0
        + (2.0 - 2.0 * np.cos(np.pi * levels / NZ))[:, None]
        + (2.0 - 2.0 * np.cos(np.pi * waves / BY))[None, :]
    )
    factors = [np.zeros((NZ, BY))]
    for _ in range(1, BX):
        factors.append(1.0 / (diagonal - factors[-1]))
    edges = np.zeros((BY, BY))
    edges[:, 0] = edge_rows[:, 1]
    edges[0, 0] = 1.0
    edges[:, BX] = edge_rows[:, BY - 1]
    near = sines[1].copy()
    far = sines[BY - 1].copy()
    return dict(
        vertical=left_stack(vertical),
        vertical_right=right_stack(vertical),
        to_waves=right_stack(-4.0 * to_waves),
        plain_sines=right_stack(sines),
        edge_rows=right_stack(edge_rows),
        from_waves=right_stack(from_waves),
        edges=right_stack(edges),
        factors=np.stack(factors[1:]).astype(np.float32),
        near_far=np.stack([near, far] + [np.zeros(BY)] * 6).astype(np.float32),
    )


def skeleton_tables():
    total_x, total_y = CX * BX, RY * BY
    grid = np.zeros((RY, CX, CX, RY))
    a0, c = np.arange(CX), np.arange(CX)
    b0, r = np.arange(RY), np.arange(RY)
    part_x = cas(2 * np.pi * np.outer(a0, c) / CX)
    part_y = cas(2 * np.pi * np.outer(b0, r) / RY)
    grid = np.einsum("ac,br->bacr", part_x, part_y)
    mirrored = grid[:, -a0 % CX]
    grid = grid.reshape(ND, ND)
    mirrored = mirrored.reshape(ND, ND)
    j, i = np.arange(BY), np.arange(BX)
    b1, a1 = np.arange(BY), np.arange(BX)
    y_forward, y_inverse = [], []
    for b in range(RY):
        angle = 2 * np.pi * np.outer(j, b + RY * b1) / total_y
        y_forward.append(np.concatenate([np.cos(angle), np.sin(angle)]))
        angle_other = 2 * np.pi * np.outer(j, (-b) % RY + RY * b1) / total_y
        y_inverse.append(np.concatenate([np.cos(angle).T, np.sin(angle_other).T]))
    x_forward, x_inverse = [], []
    for a in range(CX):
        angle = 2 * np.pi * np.outer(i, a + CX * a1) / total_x
        x_forward.append(np.concatenate([np.cos(angle), np.sin(angle)]))
        angle_other = 2 * np.pi * np.outer(i, (-a) % CX + CX * a1) / total_x
        x_inverse.append(np.concatenate([np.cos(angle).T, np.sin(angle_other).T]))

    def lanes(blocks):
        matrix = np.concatenate(blocks)
        out = np.concatenate(halves(matrix), axis=1)
        return np.concatenate([out, np.zeros((out.shape[0], 64), out.dtype)], axis=1)

    lane = np.arange(ND)
    lane_b0, lane_a0 = lane // CX, lane % CX
    wave_x = lane_a0[None, :] + CX * a1[:, None]
    wave_y = lane_b0[None, :] + RY * b1[:, None]
    swap = np.zeros((ND, ND))
    swap[(lane_b0 * CX + (-lane_a0) % CX), lane] = 1.0
    return dict(
        grid=left_stack(grid),
        mirrored=left_stack(mirrored),
        grid_back=left_stack(grid.T / (total_x * total_y)),
        y_forward=np.stack([wide_stack(m) for m in y_forward]),
        y_inverse=np.stack([wide_stack(m) for m in y_inverse]),
        x_forward=lanes(x_forward),
        x_inverse=lanes(x_inverse),
        swap=swap.astype(ml_dtypes.bfloat16),
        eigen_x=(2 - 2 * np.cos(2 * np.pi * wave_x / total_x)).astype(np.float32),
        eigen_y=(2 - 2 * np.cos(2 * np.pi * wave_y / total_y)).astype(np.float32),
    )


def split(values):
    high = values.astype(bf16)
    return high, (values - high.astype(f32)).astype(bf16)


def dot(left, right):
    return jnp.dot(left, right, preferred_element_type=f32)


def times_right(values, stack):
    out = dot(jnp.concatenate(split(values), axis=1), stack)
    half = out.shape[1] // 2
    return out[:, :half] + out[:, half:]


def times_left(stack, values):
    out = dot(stack, jnp.concatenate(split(values), axis=0))
    half = out.shape[0] // 2
    return out[:half] + out[half:]


def lane_index(rows):
    return lax.broadcasted_iota(jnp.int32, (rows, BY), 1)


def row_index(rows):
    return lax.broadcasted_iota(jnp.int32, (rows, BY), 0)


def edge_kernel(fields, first_x, last_x, first_y, last_y, held, west, east, south, north, *sems):
    sem, out_sem = sems

    def copy(number):
        return pltpu.make_async_copy(fields.at[number], held.at[number], sem.at[number])

    for number in range(5):
        copy(number).start()
    lane = lane_index(BX)

    def out_copies(number):
        plane = pl.ds(pl.multiple_of(number * NZ, NZ), NZ)
        groups = pl.ds(2 * number, 2)
        pairs = (
            (east.at[plane], first_x.at[plane]),
            (west.at[plane], last_x.at[plane]),
            (north.at[groups], first_y.at[groups]),
            (south.at[groups], last_y.at[groups]),
        )
        return [
            pltpu.make_async_copy(source, target, out_sem.at[4 * number + index])
            for index, (source, target) in enumerate(pairs)
        ]

    def step(number, carry):
        copy(number).wait()
        rows = held.at[number].reshape(NZ * BX, BY)
        east[pl.ds(pl.multiple_of(number * NZ, NZ), NZ), :] = rows[pl.ds(0, NZ, stride=BX), :]
        west[pl.ds(pl.multiple_of(number * NZ, NZ), NZ), :] = rows[pl.ds(BX - 1, NZ, stride=BX), :]
        for group in range(2):
            first, last = jnp.zeros((BX, BY), f32), jnp.zeros((BX, BY), f32)
            for level in range(NZ // 2):
                turned = held[number, group * (NZ // 2) + level]
                if level:
                    turned = pltpu.roll(turned, 2 * level, axis=1)
                first = jnp.where(lane == 2 * level, turned, first)
                last = jnp.where(lane == (2 * level - 1) % BY, turned, last)
            north[2 * number + group] = first
            south[2 * number + group] = last
        for copied in out_copies(number):
            copied.start()
        return carry

    lax.fori_loop(0, 5, step, 0)
    for number in range(5):
        for copied in out_copies(number):
            copied.wait()


def block_edges(fields):
    plane = (5 * NZ, BY)
    packed = (10, BX, BY)
    shapes = [plane, plane, packed, packed]
    return pl.pallas_call(
        edge_kernel,
        in_specs=[any_spec],
        out_specs=[any_spec] * 4,
        out_shape=[jax.ShapeDtypeStruct(shape, f32) for shape in shapes],
        scratch_shapes=[pltpu.VMEM((5, NZ, BX, BY), f32)]
        + [pltpu.VMEM(shape, f32) for shape in shapes]
        + [pltpu.SemaphoreType.DMA((5,)), pltpu.SemaphoreType.DMA((20,))],
        compiler_params=pltpu.CompilerParams(vmem_limit_bytes=GRANT),
    )(fields)


def eliminate(rhs, factors, reduced):
    def forward(index, reduced_prev):
        value = factors[index] * (rhs[index] + reduced_prev)
        reduced[index] = value
        return value

    zero = jnp.zeros((NZ, BY), f32)
    lax.fori_loop(0, BX - 1, forward, zero, unroll=True)

    def backward(step, above):
        index = BX - 2 - step
        value = reduced[index] + factors[index] * above
        reduced[index] = value
        return value

    lax.fori_loop(0, BX - 1, backward, zero, unroll=True)


def fetches(sources, targets, sem):
    copies = [
        pltpu.make_async_copy(source, target, sem.at[number])
        for number, (source, target) in enumerate(zip(sources, targets))
    ]
    for copy in copies:
        copy.start()
    return copies


def shapes_of(arrays):
    return [pltpu.VMEM(array.shape, array.dtype) for array in arrays]


def part_copy(source, target, sem, part):
    levels = pl.ds(part * CHUNK, CHUNK)
    pick = lambda ref: ref.at[levels] if len(ref.shape) == 3 else ref.at[:, levels]
    return pltpu.make_async_copy(pick(source), pick(target), sem.at[part])


def coefficients(u, v, w, fluid):
    carried = fluid * 0.125
    mixed = fluid * 0.025
    u_part, v_part, w_part = u * carried, v * carried, w * carried
    return (
        mixed - u_part,
        mixed + u_part,
        mixed - v_part,
        mixed + v_part,
        mixed - w_part,
        mixed + w_part,
    )


def aligned(packed, part, offset):
    return pltpu.roll(packed, lax.rem(offset + 2 * BY - part * CHUNK, BY), axis=1)


def turned_back(value, sub):
    return pltpu.roll(value, BY - sub, axis=1) if sub else value


def merged_sides(south, north, sides, numbers):
    even = lax.rem(lane_index(BX), 2) == 0
    for number in numbers:
        for index in (2 * number, 2 * number + 1):
            sides[index] = jnp.where(
                even,
                pltpu.roll(south[index], 1, axis=1),
                pltpu.roll(north[index], BY - 1, axis=1),
            )


def part_sides(sides, number, part):
    group = part // (PARTS // 2)
    start = 2 * CHUNK * lax.rem(part, PARTS // 2)
    return pltpu.roll(sides[2 * number + group], lax.rem(BY - start, BY), axis=1)


def neighbour_sum(ref, n, level, sub, f, up, down, side, coefs, lane):
    c_east, c_west, c_north, c_south, c_up, c_down = coefs
    f_west = ref[n, level, 7 : 7 + BX]
    f_east = ref[n, level, 9 : 9 + BX]
    side = turned_back(side, 2 * sub)
    f_north = jnp.where(lane == BY - 1, side, pltpu.roll(f, BY - 1, axis=1))
    f_south = jnp.where(lane == 0, side, pltpu.roll(f, 1, axis=1))
    return (
        (c_east * f_east + c_west * f_west)
        + (c_north * f_north + c_south * f_south)
        + (c_up * up + c_down * down)
    )


def put_rows(fields, west, east, numbers):
    for slot, number in enumerate(numbers):
        rows = fields.at[slot].reshape(NZ * ROWS, BY)
        rows[pl.ds(7, NZ, stride=ROWS), :] = west[number * NZ : (number + 1) * NZ, :]
        rows[pl.ds(8 + BX, NZ, stride=ROWS), :] = east[number * NZ : (number + 1) * NZ, :]


def near_levels(level, sub):
    below = jnp.maximum(level - 1, 0) if sub == 0 else level - 1
    above = jnp.minimum(level + 1, NZ - 1) if sub == CHUNK - 1 else level + 1
    return below, above


def source_kernel(*refs):
    fields_hbm, wall_hbm = refs[:2]
    inputs, refs = refs[2:13], refs[13:]
    new_hbm, waves_hbm, condensed_hbm = refs[:3]
    held, refs = refs[3:14], refs[14:]
    heights, west, east, south, north, to_waves = held[:6]
    vertical, vertical_right, edge_rows, edges, factors = held[6:]
    fields, wall, new, source, waves, reduced, condensed, sides, ends_x = refs[:9]
    in_sem, wall_sem, out_sem, held_sem, last_sem = refs[9:]
    copies = fetches(inputs[:6], held[:6], held_sem)

    def field_copy(part):
        levels = pl.ds(part * CHUNK, CHUNK)
        return pltpu.make_async_copy(
            fields_hbm.at[pl.ds(0, 3), levels],
            fields.at[:, levels, pl.ds(8, BX)],
            in_sem.at[part],
        )

    for part in range(PARTS):
        field_copy(part).start()
        part_copy(wall_hbm, wall, wall_sem, part).start()
    tables = fetches(inputs[6:], held[6:], held_sem.at[pl.ds(6, 5)])
    for copy in copies:
        copy.wait()
    put_rows(fields, west, east, range(3))
    merged_sides(south, north, sides, range(3))
    field_copy(0).wait()

    lane = lane_index(BX)
    row = row_index(BX)
    zero = jnp.zeros((BX, BY), f32)

    def spread(part):
        pieces = []
        ends = zero
        for sub in range(CHUNK):
            level = part * CHUNK + sub
            u, v, w = new[0, level], new[1, level], new[2, level]
            if sub:
                w_below = new[2, level - 1]
            else:
                w_below = jnp.where(part > 0, new[2, jnp.maximum(level - 1, 0)], 0.0)
            u_behind = jnp.where(row == 0, 0.0, pltpu.roll(u, 1, axis=0))
            v_behind = pltpu.roll(v, 1, axis=1)
            ends = jnp.where(lane == sub, turned_back(v_behind, BY - sub), ends)
            v_behind = jnp.where(lane == 0, 0.0, v_behind)
            divergence = (u - u_behind) + (v - v_behind) + (w - w_below)
            ends_x[pl.ds(level, 1), :] = -4.0 * divergence[:1]
            ends_x[pl.ds(NZ + level, 1), :] = 4.0 * u[BX - 1 :]
            pieces.append(divergence)
        along_y = times_right(jnp.concatenate(pieces, axis=0), to_waves[...])
        for sub in range(CHUNK):
            rows = pl.ds(part * CHUNK + sub, BX, stride=NZ)
            source[rows, :] = along_y[sub * BX : (sub + 1) * BX]
        return pltpu.roll(ends, part * CHUNK, axis=1)

    def part_step(part, v_edge):
        @pl.when(part < PARTS - 1)
        def _():
            field_copy(part + 1).wait()

        part_copy(wall_hbm, wall, wall_sem, part).wait()
        v_edge = v_edge + jnp.where(part > 0, spread(jnp.maximum(part - 1, 0)), 0.0)
        turned = [part_sides(sides, n, part) for n in range(3)]
        for sub in range(CHUNK):
            level = part * CHUNK + sub
            below, above = near_levels(level, sub)
            u, v, w = [fields[n, level, 8 : 8 + BX] for n in range(3)]
            fluid = jnp.where(level >= heights[...], 1.0, 0.0).astype(f32)
            coefs = coefficients(u, v, w, fluid)
            speed = jnp.sqrt(u * u + v * v + w * w + 0.01)
            own = fluid * (0.85 - 0.2 * wall[level].astype(f32) * speed)
            for n, f in enumerate((u, v, w)):
                new[n, level] = own * f + neighbour_sum(
                    fields,
                    n,
                    level,
                    sub,
                    f,
                    fields[n, above, 8 : 8 + BX],
                    fields[n, below, 8 : 8 + BX],
                    turned[n],
                    coefs,
                    lane,
                )
        part_copy(new, new_hbm, out_sem, part).start()
        return v_edge

    v_edge = lax.fori_loop(0, PARTS, part_step, zero)

    v_edge = v_edge + spread(PARTS - 1)
    for copy in tables:
        copy.wait()
    for i in range(1, BX - 1, 2):
        pair = [source[n * NZ : (n + 1) * NZ, :] for n in (i, i + 1)]
        out = times_left(vertical[...], jnp.concatenate(pair, axis=1))
        waves[i - 1] = out[:, :BY]
        waves[i] = out[:, BY:]
    waves[BX - 2] = times_left(vertical[...], source[(BX - 1) * NZ : BX * NZ, :])
    pair = jnp.concatenate([ends_x[0:NZ, :], ends_x[NZ : 2 * NZ, :]], axis=1)
    out = times_left(vertical[...], pair)
    own_x, next_x = out[:, :BY], out[:, BY:]

    waves_copy = pltpu.make_async_copy(waves, waves_hbm, last_sem.at[0])
    waves_copy.start()
    eliminate(waves, factors, reduced)

    own_x = own_x + times_right(reduced[0], edge_rows[...])
    next_x = next_x + times_right(reduced[BX - 2], edge_rows[...])
    lane_z = lane_index(NZ)
    next_y = times_right(4.0 * v_edge[:, :NZ], vertical_right[...])
    packed = jnp.concatenate([zero[:, :NZ], next_y, jnp.zeros((2 * BX, NZ), f32)], axis=0).T
    for i in range(1, BX):
        merged = jnp.where(lane_z == 0, waves[i - 1], reduced[i - 1])
        ends = pltpu.roll(times_right(merged, edges[...]), i, axis=1)
        packed = packed + jnp.where((lane_z == i) | (lane_z == BX + i), ends, 0.0)
    condensed[pl.ds(0, NZ, stride=4), :] = own_x
    condensed[pl.ds(1, NZ, stride=4), :] = next_x
    condensed[pl.ds(2, NZ, stride=4), :] = packed
    condensed[pl.ds(3, NZ, stride=4), :] = jnp.zeros((NZ, BY), f32)
    condensed[4 * NZ :, :] = jnp.zeros((4 * (ND - NZ), BY), f32)
    condensed_copy = pltpu.make_async_copy(condensed, condensed_hbm, last_sem.at[1])
    condensed_copy.start()
    waves_copy.wait()
    condensed_copy.wait()
    for part in range(PARTS):
        part_copy(new, new_hbm, out_sem, part).wait()


vmem_spec = pl.BlockSpec(memory_space=pltpu.VMEM)
any_spec = pl.BlockSpec(memory_space=pl.ANY)


def condensed_source(fields, wall_class, heights, west, east, south, north, tables):
    names = ("to_waves", "vertical", "vertical_right", "edge_rows", "edges", "factors")
    held = [heights, west, east, south, north] + [tables[name] for name in names]
    return pl.pallas_call(
        source_kernel,
        in_specs=[any_spec] * 13,
        out_specs=[any_spec] * 3,
        out_shape=[
            jax.ShapeDtypeStruct((3, NZ, BX, BY), f32),
            jax.ShapeDtypeStruct((BX - 1, NZ, BY), f32),
            jax.ShapeDtypeStruct((4 * ND, BY), f32),
        ],
        scratch_shapes=shapes_of(held)
        + [
            pltpu.VMEM((3, NZ, ROWS, BY), f32),
            pltpu.VMEM((NZ, BX, BY), jnp.int32),
            pltpu.VMEM((3, NZ, BX, BY), f32),
            pltpu.VMEM((BX * NZ, BY), f32),
            pltpu.VMEM((BX - 1, NZ, BY), f32),
            pltpu.VMEM((BX - 1, NZ, BY), f32),
            pltpu.VMEM((4 * ND, BY), f32),
            pltpu.VMEM((10, BX, BY), f32),
            pltpu.VMEM((2 * NZ, BY), f32),
            pltpu.SemaphoreType.DMA((PARTS,)),
            pltpu.SemaphoreType.DMA((PARTS,)),
            pltpu.SemaphoreType.DMA((PARTS,)),
            pltpu.SemaphoreType.DMA((11,)),
            pltpu.SemaphoreType.DMA((2,)),
        ],
        compiler_params=pltpu.CompilerParams(vmem_limit_bytes=GRANT),
        cost_estimate=pl.CostEstimate(flops=0, bytes_accessed=40000000, transcendentals=0),
    )(fields, wall_class, *held)


def scalar_kernel(*refs):
    fields_hbm, wall_hbm = refs[:2]
    inputs, new_hbm, held, refs = refs[2:7], refs[7], refs[8:13], refs[13:]
    heights, west, east, south, north = held
    fields, scalars, wall, new, sides = refs[:5]
    in_sem, scalar_sem, wall_sem, out_sem, held_sem = refs[5:]
    copies = fetches(inputs, held, held_sem)

    def out_copy(part):
        levels = pl.ds(part * CHUNK, CHUNK)
        return pltpu.make_async_copy(
            new.at[:, levels], new_hbm.at[pl.ds(3, 2), levels], out_sem.at[part]
        )

    def in_copy(part):
        levels = pl.ds(part * CHUNK, CHUNK)
        return pltpu.make_async_copy(
            fields_hbm.at[pl.ds(0, 3), levels], fields.at[:, levels], in_sem.at[part]
        )

    def scalar_copy(part):
        levels = pl.ds(part * CHUNK, CHUNK)
        return pltpu.make_async_copy(
            fields_hbm.at[pl.ds(3, 2), levels],
            scalars.at[:, levels, pl.ds(8, BX)],
            scalar_sem.at[part],
        )

    for part in range(PARTS):
        in_copy(part).start()
        scalar_copy(part).start()
        part_copy(wall_hbm, wall, wall_sem, part).start()
    for copy in copies:
        copy.wait()
    put_rows(scalars, west, east, (3, 4))
    merged_sides(south, north, sides, (3, 4))
    scalar_copy(0).wait()
    lane = lane_index(BX)

    def part_step(part, carry):
        @pl.when(part < PARTS - 1)
        def _():
            scalar_copy(part + 1).wait()

        in_copy(part).wait()
        part_copy(wall_hbm, wall, wall_sem, part).wait()
        turned = [part_sides(sides, 3 + n, part) for n in range(2)]
        for sub in range(CHUNK):
            level = part * CHUNK + sub
            below, above = near_levels(level, sub)
            fluid = jnp.where(level >= heights[...], 1.0, 0.0).astype(f32)
            coefs = coefficients(fields[0, level], fields[1, level], fields[2, level], fluid)
            flux = fluid * (0.15 * wall[level].astype(f32))
            own = 1.0 - fluid * 0.15 - flux
            for n, target in enumerate((1.0, -0.5)):
                f = scalars[n, level, 8 : 8 + BX]
                new[n, level] = (own * f + target * flux) + neighbour_sum(
                    scalars,
                    n,
                    level,
                    sub,
                    f,
                    scalars[n, above, 8 : 8 + BX],
                    scalars[n, below, 8 : 8 + BX],
                    turned[n],
                    coefs,
                    lane,
                )
        out_copy(part).start()
        return carry

    lax.fori_loop(0, PARTS, part_step, 0)
    for part in range(PARTS):
        out_copy(part).wait()


def new_scalars(fields, wall_class, *held):
    return pl.pallas_call(
        scalar_kernel,
        in_specs=[any_spec] * 7,
        out_specs=any_spec,
        out_shape=jax.ShapeDtypeStruct((5, NZ, BX, BY), f32),
        scratch_shapes=shapes_of(held)
        + [
            pltpu.VMEM((3, NZ, BX, BY), f32),
            pltpu.VMEM((2, NZ, ROWS, BY), f32),
            pltpu.VMEM((NZ, BX, BY), jnp.int32),
            pltpu.VMEM((2, NZ, BX, BY), f32),
            pltpu.VMEM((10, BX, BY), f32),
            pltpu.SemaphoreType.DMA((PARTS,)),
            pltpu.SemaphoreType.DMA((PARTS,)),
            pltpu.SemaphoreType.DMA((PARTS,)),
            pltpu.SemaphoreType.DMA((PARTS,)),
            pltpu.SemaphoreType.DMA((5,)),
        ],
        compiler_params=pltpu.CompilerParams(vmem_limit_bytes=GRANT),
        cost_estimate=pl.CostEstimate(flops=0, bytes_accessed=30000000, transcendentals=0),
    )(fields, wall_class, *held)


def blockwise(values, stacks):
    parts = []
    for b in range(RY):
        other = (-b) % RY
        pair = jnp.concatenate(
            [values[b * CX : (b + 1) * CX], values[other * CX : (other + 1) * CX]], axis=1
        )
        out = dot(jnp.concatenate(split(pair), axis=0), stacks[b])
        parts.append(out[:CX, :BY] + out[:CX, BY:] + out[CX:, :BY])
    return jnp.concatenate(parts, axis=0)


def per_column(values, mirrored, table):
    pair = values + pltpu.roll(mirrored, BX, axis=1)
    pair = pair + pltpu.roll(pair, 2 * BX, axis=1)
    lane, row = lane_index(ND), row_index(ND)
    mine = lax.rem(row, CX)
    wide = jnp.concatenate(
        [jnp.where(mine == 2 * q + lane // 64, pair, 0.0) for q in range(CX // 2)], axis=1
    )
    out = dot(jnp.concatenate(split(wide), axis=0), table)
    top, bottom = out[:ND], out[ND:]
    out = top + pltpu.roll(top, BY - BX, axis=1) + bottom
    return jnp.where(lane < BX, out, 0.0)


skeleton_names = (
    "grid",
    "mirrored",
    "y_forward",
    "x_forward",
    "eigen_x",
    "eigen_y",
    "swap",
    "y_inverse",
    "x_inverse",
    "grid_back",
)


def skeleton_kernel(mode_eigen, *refs):
    inputs, answer_hbm, held, refs = refs[:11], refs[11], refs[12:23], refs[23:]
    received, grid, mirrored, y_forward, x_forward, eigen_x, eigen_y = held[:7]
    swap, y_inverse, x_inverse, grid_back = held[7:]
    answer, held_sem, last_sem = refs
    copies = fetches(inputs, held, held_sem)
    def wait(first, last):
        for copy in copies[first:last]:
            copy.wait()

    wait(0, 3)
    own_x = received[pl.ds(0, ND, stride=4), :]
    next_x = received[pl.ds(1, ND, stride=4), :]
    lines_y = received[pl.ds(2, ND, stride=4), :]
    lane = lane_index(ND)
    lines_x = own_x + pltpu.roll(next_x, RY, axis=0)
    before = pltpu.roll(lines_y, BY - BX, axis=1).reshape(CX, RY, BY)
    before = pltpu.roll(before, 1, axis=1).reshape(ND, BY)
    lines_y = jnp.where(lane < BX, lines_y + before, 0.0)

    both = times_left(grid[...], jnp.concatenate([lines_x, lines_y], axis=1))
    turned = times_left(mirrored[...], lines_y)
    wait(3, 4)
    spec_x = blockwise(both[:, :BY], y_forward).T
    wait(4, 7)
    spec_y = per_column(both[:, BY:], turned, x_forward[...]).T

    base = eigen_y[...] + mode_eigen[0]
    total_x = jnp.zeros((BY, ND), f32)
    sums = []
    for a in range(BX):
        value = (spec_x + spec_y[a : a + 1]) / (base + eigen_x[a : a + 1])
        total_x = total_x + value
        sums.append(jnp.sum(value, axis=0, keepdims=True))
    total_y = jnp.concatenate(sums, axis=0)
    high, low = split(total_y)
    wait(7, 11)
    turned = dot(high, swap[...]) + dot(low, swap[...])
    fill = jnp.zeros((ND - BX, ND), f32)
    total_y = jnp.concatenate([total_y, fill], axis=0).T
    turned = jnp.concatenate([turned, fill], axis=0).T
    lines_x = blockwise(total_x.T, y_inverse)
    lines_y = per_column(total_y, turned, x_inverse[...])
    both = times_left(grid_back[...], jnp.concatenate([lines_x, lines_y], axis=1))
    own_x, own_y = both[:, :BY], both[:, BY:]
    next_x = pltpu.roll(own_x, ND - RY, axis=0)
    next_y = pltpu.roll(own_y.reshape(CX, RY, BY), RY - 1, axis=1).reshape(ND, BY)
    answer[pl.ds(0, ND, stride=4), :] = own_x
    answer[pl.ds(1, ND, stride=4), :] = next_x
    answer[pl.ds(2, ND, stride=4), :] = own_y + pltpu.roll(next_y, BX, axis=1)
    answer[pl.ds(3, ND, stride=4), :] = jnp.zeros((ND, BY), f32)
    answer_copy = pltpu.make_async_copy(answer, answer_hbm, last_sem.at[0])
    answer_copy.start()
    answer_copy.wait()


def skeleton_solve(received, mode_eigen, tables):
    held = [received] + [tables[name] for name in skeleton_names]
    return pl.pallas_call(
        skeleton_kernel,
        in_specs=[pl.BlockSpec(memory_space=pltpu.SMEM)] + [any_spec] * 11,
        out_specs=any_spec,
        out_shape=jax.ShapeDtypeStruct((4 * ND, BY), f32),
        scratch_shapes=shapes_of(held)
        + [
            pltpu.VMEM((4 * ND, BY), f32),
            pltpu.SemaphoreType.DMA((11,)),
            pltpu.SemaphoreType.DMA((1,)),
        ],
        compiler_params=pltpu.CompilerParams(vmem_limit_bytes=GRANT),
    )(mode_eigen, *held)


correct_names = (
    "factors",
    "plain_sines",
    "near_far",
    "vertical",
    "vertical_right",
    "from_waves",
)


def correct_kernel(*refs):
    before_hbm, inputs = refs[0], refs[1:10]
    new_hbm, pressure_hbm, held, refs = refs[11], refs[12], refs[13:22], refs[22:]
    answer, waves, factors, plain_sines, near_far = held[:5]
    vertical, vertical_right, from_waves, heights = held[5:]
    velocity, pressure, reduced, in_sem, out_sem, pressure_sem, held_sem, row_sem = refs
    first = [pl.ds(0, 8), pl.ds(8, 8), pl.ds(16, BX - 17)]
    copies = fetches(inputs[:1], held[:1], held_sem)
    rows_in = []
    for number, rows in enumerate(first):
        pair = [inputs[1].at[rows], inputs[2].at[rows]]
        held_pair = [waves.at[rows], factors.at[rows]]
        rows_in.append(fetches(pair, held_pair, row_sem.at[pl.ds(2 * number, 2)]))
    copies += fetches(inputs[3:], held[3:], held_sem.at[pl.ds(1, 6)])

    def pressure_copy(part):
        levels = pl.ds(part * CHUNK, CHUNK)
        return pltpu.make_async_copy(
            pressure.at[levels, pl.ds(0, BX)], pressure_hbm.at[levels], pressure_sem.at[part]
        )

    def out_copy(part):
        levels = pl.ds(part * CHUNK, CHUNK)
        return pltpu.make_async_copy(
            velocity.at[:, levels], new_hbm.at[pl.ds(0, 3), levels], out_sem.at[part]
        )

    for copy in copies[:3]:
        copy.wait()
    for part in range(PARTS):
        part_copy(before_hbm, velocity, in_sem, part).start()
    own_x = answer[pl.ds(0, NZ, stride=4), :]
    next_x = answer[pl.ds(1, NZ, stride=4), :]
    lines_y = answer[pl.ds(2, NZ, stride=4), :]
    lane_z = lane_index(NZ)
    near, far = near_far[0:1], near_far[1:2]
    for i in range(1, BX):
        if i in (1, 9, 17):
            for copy in rows_in[i // 8]:
                copy.wait()
        rhs = waves[i - 1] + lines_y[:, i : i + 1] * near + lines_y[:, BX + i : BX + i + 1] * far
        if i == 1:
            rhs = rhs + times_right(own_x, plain_sines[...])
        if i == BX - 1:
            rhs = rhs + times_right(next_x, plain_sines[...])
        reduced[i - 1] = rhs
    eliminate(reduced, factors, reduced)

    for copy in copies[3:]:
        copy.wait()
    rows = pressure.reshape(NZ * TALL, BY)
    planes = [own_x]
    for i in range(1, BX):
        merged = jnp.where(lane_z == 0, lines_y[:, i : i + 1], reduced[i - 1])
        planes.append(times_right(merged, from_waves[...]))
        if i % 2:
            out = times_left(vertical[...], jnp.concatenate(planes, axis=1))
            rows[pl.ds(i - 1, NZ, stride=TALL), :] = out[:, :BY]
            rows[pl.ds(i, NZ, stride=TALL), :] = out[:, BY:]
            planes = []
    rows[pl.ds(BX, NZ, stride=TALL), :] = times_left(vertical[...], next_x)
    tall = jnp.concatenate([lines_y, jnp.zeros((BY - NZ, BY), f32)], axis=0).T
    north = times_right(tall[BX : 2 * BX, :NZ], vertical_right[...])
    north = jnp.concatenate([north, jnp.zeros((BX, BY - NZ), f32)], axis=1)

    lane = lane_index(BX)

    def part_step(part, here):
        part_copy(before_hbm, velocity, in_sem, part).wait()
        sides = aligned(north, part, BY - 1)
        for sub in range(CHUNK):
            level = part * CHUNK + sub
            _, above_level = near_levels(level, sub)
            above = pressure[above_level, 0:BX]
            if sub == CHUNK - 1:
                above = jnp.where(level == NZ - 1, -here, above)
            east = pressure[level, 1 : BX + 1]
            side = jnp.where(
                lane == BY - 1, turned_back(sides, sub), pltpu.roll(here, BY - 1, axis=1)
            )
            factor = jnp.where(level >= heights[...], 0.25, 0.0).astype(f32)
            velocity[0, level] = velocity[0, level] - factor * (east - here)
            velocity[1, level] = velocity[1, level] - factor * (side - here)
            velocity[2, level] = velocity[2, level] - factor * (above - here)
            here = above
        out_copy(part).start()
        pressure_copy(part).start()
        return here

    lax.fori_loop(0, PARTS, part_step, pressure[0, 0:BX])
    for part in range(PARTS):
        out_copy(part).wait()
        pressure_copy(part).wait()


def corrected(before, waves, answer, heights, scalars, tables):
    held = [answer, waves] + [tables[name] for name in correct_names] + [heights]
    return pl.pallas_call(
        correct_kernel,
        in_specs=[any_spec] * 11,
        out_specs=[any_spec, any_spec],
        out_shape=[
            jax.ShapeDtypeStruct((5, NZ, BX, BY), f32),
            jax.ShapeDtypeStruct((NZ, BX, BY), f32),
        ],
        scratch_shapes=shapes_of(held)
        + [
            pltpu.VMEM((3, NZ, BX, BY), f32),
            pltpu.VMEM((NZ, TALL, BY), f32),
            pltpu.VMEM((BX - 1, NZ, BY), f32),
            pltpu.SemaphoreType.DMA((PARTS,)),
            pltpu.SemaphoreType.DMA((PARTS,)),
            pltpu.SemaphoreType.DMA((PARTS,)),
            pltpu.SemaphoreType.DMA((7,)),
            pltpu.SemaphoreType.DMA((6,)),
        ],
        input_output_aliases={10: 0},
        compiler_params=pltpu.CompilerParams(vmem_limit_bytes=GRANT),
    )(before, *held, scalars)


def ring(value, axis, step):
    count = lax.axis_size(axis)
    return lax.ppermute(value, axis, [(n, (n + step) % count) for n in range(count)])


def exchanged(value):
    value = value.reshape(ND, 4, BY)
    return lax.all_to_all(value, ("col", "row"), 0, 0, tiled=True).reshape(4 * ND, BY)


def on_device(fields, heights, wall_class):
    block = {name: jnp.asarray(table) for name, table in block_tables().items()}
    skeleton = {name: jnp.asarray(table) for name, table in skeleton_tables().items()}
    first_x, last_x, first_y, last_y = block_edges(fields)
    west = ring(last_x, "col", 1)
    east = ring(first_x, "col", -1)
    south = ring(last_y, "row", 1)
    north = ring(first_y, "row", -1)
    before, waves, condensed = condensed_source(
        fields, wall_class, heights, west, east, south, north, block
    )
    received = exchanged(condensed)
    scalars = new_scalars(fields, wall_class, heights, west, east, south, north)
    mode = lax.axis_index("col") * RY + lax.axis_index("row")
    eigen = 2.0 - 2.0 * np.cos(np.pi * (np.arange(ND) + 0.5) / NZ)
    eigen[NZ:] = 1.0
    mode_eigen = lax.dynamic_slice(jnp.asarray(eigen.astype(np.float32)), (mode,), (1,))
    solved = skeleton_solve(received, mode_eigen, skeleton)
    answer = exchanged(solved)
    return tuple(corrected(before, waves, answer, heights, scalars, block))


def solution(mesh):
    in_specs = (P(None, None, "col", "row"), P("col", "row"), P(None, "col", "row"))
    out_specs = (P(None, None, "col", "row"), P(None, "col", "row"))
    return jax.shard_map(
        on_device, mesh=mesh, in_specs=in_specs, out_specs=out_specs, check_vma=False
    )
```
